32 devices in a mesh: groups: 2 (over y), expert: 4 (over z), dp: 4 (over x, core).
Axes of the slice: x: 2, y: 2, z: 4, core: 2. Of those that a mesh axis runs over, the one named last changes fastest.
Arguments:
- routes: int32 [4096, 8], P(('groups', 'expert', 'dp')), parts along dimension 0, may hold values from 0 to 63, all different within a row; in each aligned block of 128 rows (0 to 127, 128 to 255, ...) at most 18 rows name the same one
- combine: bfloat16 [4096, 8], P(('groups', 'expert', 'dp')), parts along dimension 0, may hold values from 0.019897461 to 0.29882812
- hidden: bfloat16 [4096, 8, 768], P(('groups', 'expert', 'dp')), parts along dimension 0, may hold values from -6 to 6
- d_out: bfloat16 [4096, 2048], P(('groups', 'expert', 'dp')), parts along dimension 0, may hold values from -0.1796875 to 0.1796875
- w_down: bfloat16 [64, 768, 2048], P('expert', 'dp'), may hold values from -0.21875 to 0.21875
Outputs:
- d_w_down: bfloat16 [128, 768, 2048], P(('groups', 'expert'), 'dp'), parts along dimension 0
- d_combine: float32 [4096, 8], P(('groups', 'expert', 'dp')), parts along dimension 0
The draws below stay inside these ranges and needn't reach their ends.
There are 2 independent parts, one for each index of `groups`. The reference program is written for one: setup_inputs(seed, part) draws one part's arguments, and reference() takes and returns one part's arrays. A program takes and returns all parts, laid end to end along the dimension named above; an argument that names none is the same for every part. Nothing has to cross between parts.
Inputs may be any that keep to these rules, and one draw needn't show every extreme that they name: `routes`: each row names 8 different experts, and every expert is named somewhere. Within the rows of one device (each aligned block of 128 rows) no expert is named more than 18 times, a bound that some block reaches.
All inputs are finite; a program needn't handle non-finite values.
Results may differ from the reference program's by a relative error of at most 0.012.
Values may be sent and summed in bfloat16 or wider, within the bound.
No kernel may reach another device: no remote copies, remote signals or barrier semaphores. Data moves between devices by JAX's collectives and lax.ppermute only.
A program may use at most 384 MiB of HBM per device.

```python
import math
import jax
import jax.numpy as jnp
import numpy as np
from jax import lax

D = 2048
FF = 768
EXPERTS = 64
TOPK = 8
TOK_DEV = 128
MOST = 18
TOKENS = 2048
N_EXPERT = 4
N_DP = 4


def level_of(own_key, extent, cuts, smallest, largest):
    level, own = 1.0, jax.random.fold_in(own_key, 6)
    for dim, blocks in cuts:
        draws = jnp.exp(jax.random.uniform(jax.random.fold_in(own, dim), (blocks,), jnp.float32, smallest / len(cuts), largest / len(cuts)))
        level = level * jnp.repeat(draws, extent[dim] // blocks).reshape([-1 if axis == dim else 1 for axis in range(len(extent))])
    return level


def shared_out(stream_key, own, number, rows, amount, top, most, skew):
    sequence = jax.random.permutation(stream_key, amount)
    crowded, usual = portions_of(amount, rows * top, most, skew, True), portions_of(amount, rows * top, most, skew, False)
    places = jnp.arange(amount)

    def named(sizes, turn):
        used = int((sizes > 0).sum())
        fixed = max(1, used // 4)
        moved = fixed + (places - fixed + turn * (used - fixed)) % max(1, amount - fixed)
        return jnp.zeros((amount,), jnp.int32).at[sequence[jnp.where(places < fixed, places, moved)]].set(jnp.asarray(sizes, jnp.int32))

    sizes = jnp.where(number % 4 == 0, named(crowded, number // 4), named(usual, number - number // 4 - 1))
    mixed = jax.random.permutation(jax.random.fold_in(own, 3), amount)
    source_of, receiver = mixed[0:amount // 2 * 2:2], mixed[1:amount // 2 * 2:2]
    margin = jnp.minimum(sizes[source_of] - 1, most - sizes[receiver]) // 2
    margin = jnp.where((source_of == sequence[0]) | (receiver == sequence[0]) | (sizes[receiver] == 0), 0, jnp.maximum(margin, 0))
    moved = jax.random.randint(jax.random.fold_in(own, 4), (amount // 2,), 0, 1 << 20) % (margin + 1)
    sizes = sizes.at[source_of].add(-moved).at[receiver].add(moved)
    items = jnp.searchsorted(jnp.cumsum(sizes), jnp.arange(rows * top), side="right").astype(jnp.int32)
    table = items.reshape(top, rows).T
    table = table[jax.random.permutation(jax.random.fold_in(own, 1), rows)]
    turn = jax.random.randint(jax.random.fold_in(own, 2), (rows, 1), 0, top)
    return jnp.take_along_axis(table, (jnp.arange(top)[None, :] + turn) % top, axis=1)


def portions_of(number_of, total, limit, skew, full):
    portions = [(1 << 20) // math.isqrt(standing ** skew) + 1 for standing in range(1, number_of + 1)]
    largest = limit if full else min(limit, max(-(-total // number_of), total * portions[0] // sum(portions)))
    least = 1 if total - largest >= number_of - 1 else 0
    given, spare = [largest] + [least] * (number_of - 1), total - largest - least * (number_of - 1)
    while spare > 0:
        movable = [i for i in range(1, number_of) if given[i] < largest] or [i for i in range(1, number_of) if given[i] < limit]
        pool, remaining = sum([portions[i] for i in movable]), spare
        for i in movable:
            extra = min(limit - given[i], max(1, remaining * portions[i] // pool), spare)
            given[i] = given[i] + extra
            spare = spare - extra
    return np.array(given)


def gaussian(own_key, shape, width, reach, pieces=(), held_as=jnp.bfloat16):
    array = jax.random.normal(own_key, shape, jnp.float32) * width
    if len(pieces) > 0:
        array = level_of(own_key, shape, pieces, -0.22, 0.18) * array
    return jnp.clip(array, min=-reach, max=reach).astype(held_as)


def setup_inputs(seed: int = 0, part: int = 0) -> dict:
    splits = jax.random.split(jax.random.key(seed), 6)
    part_splits = jax.random.split(jax.random.fold_in(splits[5], part), 6)
    routes_keys = jax.random.split(jax.random.fold_in(part_splits[0], 1), TOKENS // TOK_DEV)
    routes_turns = jax.random.permutation(jax.random.fold_in(part_splits[0], 3), TOKENS // TOK_DEV)
    routes = jax.vmap(lambda own, number: shared_out(jax.random.fold_in(part_splits[0], 2), own, number, TOK_DEV, EXPERTS, TOPK, MOST, 1))(routes_keys, routes_turns).reshape((TOKENS, TOPK))
    combine = jnp.clip(jnp.exp(math.log(0.29882812) - 2.7092764 * jax.random.uniform(part_splits[1], (TOKENS, TOPK), jnp.float32) ** level_of(part_splits[1], (TOKENS, TOPK), ((0, 16),), -0.2, 0.2)), 0.019897461, 0.29882812).astype(jnp.bfloat16)
    hidden = gaussian(part_splits[2], (TOKENS, TOPK, FF), 1.0, 6.0, ((0, 16),))
    d_out = gaussian(part_splits[3], (TOKENS, D), 0.03, 0.1796875, ((0, 16),))
    w_down = gaussian(splits[4], (EXPERTS, FF, D), FF ** -0.5, 0.21875, ((0, 4), (1, 4)))
    return dict(routes=routes, combine=combine, hidden=hidden, d_out=d_out, w_down=w_down)


def reference(routes, combine, hidden, d_out, w_down):
    blocks = N_EXPERT * N_DP
    n_routes = TOKENS * TOPK
    block_routes = routes.reshape(blocks, TOK_DEV * TOPK)
    numbers = jnp.arange(EXPERTS, dtype=jnp.int32)

    def block_slots(one_block):
        onehot = (one_block[:, None] == numbers[None, :]).astype(jnp.int32)
        return jnp.sum((jnp.cumsum(onehot, axis=0) - 1) * onehot, axis=1).astype(jnp.int32)

    slots = lax.map(block_slots, block_routes)
    block_ids = jnp.broadcast_to(jnp.arange(blocks, dtype=jnp.int32)[:, None], slots.shape)
    position = (block_ids * MOST + slots).astype(jnp.int32)
    route_ids = jnp.arange(n_routes, dtype=jnp.int32).reshape(blocks, TOK_DEV * TOPK)
    table = jnp.full((EXPERTS, blocks * MOST), n_routes, jnp.int32).at[block_routes, position].set(route_ids)
    hidden_flat = hidden.reshape(n_routes, FF)
    combine_flat = combine.reshape(n_routes)

    def one_expert(pair):
        ids, weights = pair
        h_rows = jnp.take(hidden_flat, ids, axis=0, mode="fill", fill_value=0)
        g_rows = jnp.take(d_out, ids // TOPK, axis=0, mode="fill", fill_value=0)
        p_rows = jnp.take(combine_flat, ids, axis=0, mode="fill", fill_value=0)
        back = jnp.dot(g_rows, weights.T, preferred_element_type=jnp.float32)
        probs_grad = jnp.sum(h_rows.astype(jnp.float32) * back, axis=1)
        scaled = (p_rows.astype(jnp.float32)[:, None] * g_rows.astype(jnp.float32)).astype(jnp.bfloat16)
        h_four = h_rows.reshape(N_EXPERT, N_DP, MOST, FF).astype(jnp.float32)
        s_four = scaled.reshape(N_EXPERT, N_DP, MOST, D).astype(jnp.float32)
        partial_sums = jnp.einsum("sdmf,sdmj->dfj", h_four, s_four).astype(jnp.bfloat16)
        total = jnp.sum(partial_sums.astype(jnp.float32), axis=0).astype(jnp.bfloat16)
        return total, probs_grad

    d_w_down, slot_grads = lax.map(one_expert, (table, w_down))
    d_combine = slot_grads[block_routes.reshape(-1), position.reshape(-1)].reshape(TOKENS, TOPK)
    return d_w_down, d_combine
```

```python
import functools

import jax
import jax.numpy as jnp
from jax import lax
from jax.experimental import pallas as pl
from jax.experimental.pallas import tpu as pltpu
from jax.sharding import PartitionSpec as P

MOST = 18
SUPER = 8
TILES = 9
GROUP = ("expert", "dp")
f32, bf16, i32 = jnp.float32, jnp.bfloat16, jnp.int32


def dot(a, b, dims=((1,), (0,))):
    return lax.dot_general(a, b, (dims, ((), ())), preferred_element_type=f32)


def iota(shape, dim):
    return lax.broadcasted_iota(i32, shape, dim)


def params(megabytes):
    return pltpu.CompilerParams(vmem_limit_bytes=megabytes * 2**20)


def cost(flops, nbytes):
    return pl.CostEstimate(flops=int(flops), bytes_accessed=int(nbytes), transcendentals=0)


def token_slots(routes_t, experts):
    top_k, tok = routes_t.shape
    numbers = iota((experts, tok), 0)
    named = jnp.zeros((experts, tok), f32)
    for k in range(top_k):
        named += jnp.where(routes_t[k : k + 1, :] == numbers, 1.0, 0.0)
    before = jnp.where(iota((tok, tok), 0) < iota((tok, tok), 1), 1.0, 0.0)
    return named, dot(named.astype(bf16), before.astype(bf16))


def pack_kernel(n_dp, half, routes_t, routes_flat, weights_flat, hidden, out, target):
    ex = pl.program_id(0)
    experts = pl.num_programs(0) * 2 * half // MOST
    n_routes = routes_flat.shape[1]
    top_k, tok = routes_t.shape
    units = hidden.shape[1]
    part = units // n_dp

    @pl.when(ex == 0)
    def _():
        _, slots = token_slots(routes_t[...], experts)
        shape = (tok, n_routes)
        spread = jnp.where(iota(shape, 1) // top_k == iota(shape, 0), 1.0, 0.0)
        slots = dot(slots.astype(bf16), spread.astype(bf16))
        numbers = iota((experts, n_routes), 0)
        rows = slots + (numbers * MOST).astype(f32)
        rows = jnp.where(routes_flat[...] == numbers, rows, 0.0)
        target[...] = jnp.sum(rows, axis=0, keepdims=True).astype(i32)

    weights = weights_flat[...].astype(f32)
    for side in range(2):
        first = ex * 2 * half + side * half
        chosen = target[...] - first == iota((half, n_routes), 0)
        chosen = jnp.where(chosen, weights, 0.0).astype(bf16)
        rows = dot(chosen, hidden[...]).astype(bf16)
        for d in range(n_dp):
            out[d, :, side * part : (side + 1) * part] = rows[:, d * part : (d + 1) * part]


def pack(routes_t, routes_flat, weights_flat, hidden, n_expert, n_dp, half):
    n_routes, units = hidden.shape
    part = units // n_dp
    whole = lambda shape: pl.BlockSpec(shape, lambda i: (0,) * len(shape))
    return pl.pallas_call(
        functools.partial(pack_kernel, n_dp, half),
        grid=(n_expert,),
        in_specs=[
            whole(routes_t.shape),
            whole(routes_flat.shape),
            whole(weights_flat.shape),
            whole(hidden.shape),
        ],
        out_specs=pl.BlockSpec((n_dp, half, 2 * part), lambda i: (i, 0, 0)),
        out_shape=jax.ShapeDtypeStruct((n_expert * n_dp, half, 2 * part), bf16),
        scratch_shapes=[pltpu.VMEM((1, n_routes), i32)],
        compiler_params=params(40),
        cost_estimate=cost(4 * n_expert * half * n_routes * units, 6 * n_routes * units),
    )(routes_t, routes_flat, weights_flat, hidden)


def tile_rows(i, rows):
    first = min(16 * i // MOST, SUPER - 2)
    place = 16 * i + iota((rows, 1), 0) % 16
    second = place >= MOST * (first + 1)
    slot = place - MOST * first - jnp.where(second, MOST, 0)
    return first, second, slot


def gather_kernel(ex_local, routes_t, grads, out):
    tok = routes_t.shape[2]
    width = grads.shape[1]
    rows = 16 * ex_local
    slots = []
    for b in range(SUPER):
        named, before = token_slots(routes_t[b], ex_local)
        slots.append(jnp.where(named > 0, before, -1.0))
    shape = (rows, ex_local)
    spread = jnp.where(iota(shape, 0) // 16 == iota(shape, 1), 1.0, 0.0).astype(bf16)
    step = min(512, width)
    for i in range(TILES):
        first, second, slot = tile_rows(i, rows)
        pair = jnp.concatenate([slots[first], slots[first + 1]], axis=1)
        pair = dot(spread, pair.astype(bf16))
        slot = slot.astype(f32)
        wanted = jnp.where(
            iota((rows, 2 * tok), 1) < tok,
            jnp.where(second, -5.0, slot),
            jnp.where(second, slot, -5.0),
        )
        chosen = jnp.where(pair == wanted, 1.0, 0.0).astype(bf16)
        for c in range(0, width, step):
            found = dot(chosen, grads[first * tok : (first + 2) * tok, c : c + step])
            found = found.astype(bf16).reshape(ex_local, 16, step)
            out[:, 16 * i : 16 * i + 16, c : c + step] = found


def gather(routes_t, grads, ex_local):
    blocks, top_k, tok = routes_t.shape
    width = grads.shape[1]
    return pl.pallas_call(
        functools.partial(gather_kernel, ex_local),
        grid=(blocks // SUPER,),
        in_specs=[
            pl.BlockSpec((SUPER, top_k, tok), lambda s: (s, 0, 0)),
            pl.BlockSpec((SUPER * tok, width), lambda s: (s, 0)),
        ],
        out_specs=pl.BlockSpec((ex_local, SUPER * MOST, width), lambda s: (0, s, 0)),
        out_shape=jax.ShapeDtypeStruct((ex_local, blocks * MOST, width), bf16),
        compiler_params=params(48),
        cost_estimate=cost(
            4 * ex_local * blocks * MOST * tok * width,
            2 * width * blocks * (tok + ex_local * MOST),
        ),
    )(routes_t, grads)


def back_kernel(grads, weights, out):
    out[0] = dot(grads[0], weights[0], ((1,), (1,)))


def back(grads, weights):
    ex_local, rows, width = grads.shape
    part = weights.shape[1]
    chunk = min(rows, 16 * MOST)
    return pl.pallas_call(
        back_kernel,
        grid=(ex_local, rows // chunk),
        in_specs=[
            pl.BlockSpec((1, chunk, width), lambda e, c: (e, c, 0)),
            pl.BlockSpec((1, part, width), lambda e, c: (e, 0, 0)),
        ],
        out_specs=pl.BlockSpec((1, chunk, part), lambda e, c: (e, c, 0)),
        out_shape=jax.ShapeDtypeStruct((ex_local, rows, part), f32),
        compiler_params=params(32),
        cost_estimate=cost(
            2 * ex_local * rows * width * part, 2 * ex_local * (rows + part) * width
        ),
    )(grads, weights)


def arrange_kernel(ex_local, received, backs, out, sums):
    blocks, half, double = received.shape
    part = double // 2
    paired = ex_local % 2 == 0
    some = ex_local // 2 if paired else ex_local
    rows = 16 * some
    for i in range(TILES):
        first, second, slot = tile_rows(i, rows)
        expert = iota((rows, 1), 0) // 16
        block = jnp.where(second, half, 0)
        source = jnp.concatenate([received[first], received[first + 1]], axis=0)
        lane = iota((rows, 128), 1)
        results = []
        for side in range(1 if paired else 2):
            place = expert * MOST + slot - side * half
            inside = (place >= 0) & (place < half)
            column = jnp.where(inside, block + place, -1)
            chosen = iota((rows, 2 * half), 1) == column
            results.append(dot(jnp.where(chosen, 1.0, 0.0).astype(bf16), source))
        if paired:
            sides = [results[0][:, :part], results[0][:, part:]]
        else:
            sides = [results[0][:, :part] + results[1][:, part:]]
        for s, piece in enumerate(sides):
            here = slice(s * some, (s + 1) * some)
            out[here, 16 * i : 16 * i + 16, :] = piece.astype(bf16).reshape(some, 16, part)
            near = backs[here, 16 * i : 16 * i + 16, :].reshape(rows, part)
            total = jnp.sum(piece * near, axis=1, keepdims=True)
            hit = lane == slot
            for b in range(2):
                mine = hit & (second if b else jnp.logical_not(second))
                found = jnp.where(mine, total, 0.0).reshape(some, 16, 128)
                found = jnp.sum(found, axis=1)
                fresh = 16 * i <= MOST * (first + b)
                if not fresh:
                    found += sums[first + b, here, :]
                sums[first + b, here, :] = found


def arrange(received, backs):
    blocks, half, double = received.shape
    ex_local, rows, part = backs.shape
    return pl.pallas_call(
        functools.partial(arrange_kernel, ex_local),
        grid=(blocks // SUPER,),
        in_specs=[
            pl.BlockSpec((SUPER, half, double), lambda s: (s, 0, 0)),
            pl.BlockSpec((ex_local, SUPER * MOST, part), lambda s: (0, s, 0)),
        ],
        out_specs=[
            pl.BlockSpec((ex_local, SUPER * MOST, part), lambda s: (0, s, 0)),
            pl.BlockSpec((SUPER, ex_local, 128), lambda s: (s, 0, 0)),
        ],
        out_shape=[
            jax.ShapeDtypeStruct((ex_local, rows, part), bf16),
            jax.ShapeDtypeStruct((blocks, ex_local, 128), f32),
        ],
        compiler_params=params(32),
        cost_estimate=cost(
            4 * ex_local * rows * half * double, ex_local * rows * part * 8
        ),
    )(received, backs)


def outer_kernel(hidden, grads, out, *scratch):
    found = dot(hidden[0], grads[0], ((0,), (0,)))
    if not scratch:
        out[0] = found.astype(bf16)
        return
    total, chunk = scratch[0], pl.program_id(1)

    @pl.when(chunk == 0)
    def _():
        total[...] = found

    @pl.when(chunk > 0)
    def _():
        total[...] += found

    @pl.when(chunk == pl.num_programs(1) - 1)
    def _():
        out[0] = total[...].astype(bf16)


def outer(hidden, grads):
    ex_local, rows, part = hidden.shape
    width = grads.shape[2]
    chunk = min(rows, 16 * MOST)
    return pl.pallas_call(
        outer_kernel,
        grid=(ex_local, rows // chunk),
        in_specs=[
            pl.BlockSpec((1, chunk, part), lambda e, c: (e, c, 0)),
            pl.BlockSpec((1, chunk, width), lambda e, c: (e, c, 0)),
        ],
        out_specs=pl.BlockSpec((1, part, width), lambda e, c: (e, 0, 0)),
        out_shape=jax.ShapeDtypeStruct((ex_local, part, width), bf16),
        scratch_shapes=[] if rows == chunk else [pltpu.VMEM((part, width), f32)],
        compiler_params=params(32),
        cost_estimate=cost(
            2 * ex_local * rows * width * part, 2 * ex_local * (rows + part) * width
        ),
    )(hidden, grads)


def finish_kernel(routes_t, weights_t, sums, out):
    experts = sums.shape[0]
    top_k, tok = routes_t.shape
    _, slots = token_slots(routes_t[...], experts)
    slots = slots.astype(i32)
    found = jnp.zeros((experts, tok), f32)
    for m in range(MOST):
        found = jnp.where(slots == m, sums[:, m : m + 1], found)
    numbers = iota((experts, tok), 0)
    for k in range(top_k):
        mine = jnp.where(routes_t[k : k + 1, :] == numbers, found, 0.0)
        total = jnp.sum(mine, axis=0, keepdims=True)
        out[k : k + 1, :] = total / weights_t[k : k + 1, :]


def finish(routes_t, weights_t, sums):
    return pl.pallas_call(
        finish_kernel,
        out_shape=jax.ShapeDtypeStruct(routes_t.shape, f32),
        cost_estimate=cost(10000, 100000),
    )(routes_t, weights_t, sums)


def body(routes, combine, hidden, d_out, w_down):
    n_expert = lax.axis_size("expert")
    n_dp = lax.axis_size("dp")
    ex_local = w_down.shape[0]
    experts = n_expert * ex_local
    tok, top_k = routes.shape
    blocks = n_expert * n_dp
    half = ex_local * MOST // 2
    routes_t = routes.T
    n_routes = tok * top_k
    grads = lax.all_gather(d_out, GROUP, axis=0, tiled=True)
    mine = jnp.broadcast_to(routes_t[None], (blocks, top_k, tok))
    all_routes = lax.all_to_all(mine, GROUP, split_axis=0, concat_axis=0, tiled=True)
    all_routes = all_routes - lax.axis_index("expert") * ex_local
    sent = pack(
        routes_t,
        routes.reshape(1, n_routes),
        combine.reshape(1, n_routes),
        hidden.reshape(n_routes, hidden.shape[2]),
        n_expert,
        n_dp,
        half,
    )
    received = lax.all_to_all(sent, GROUP, split_axis=0, concat_axis=0, tiled=True)
    grads = gather(all_routes, grads, ex_local)
    backs = back(grads, w_down)
    arranged, sums = arrange(received, backs)
    returned = lax.all_to_all(sums, GROUP, split_axis=0, concat_axis=0, tiled=True)
    d_w_down = outer(arranged, grads)
    returned = jnp.sum(returned.reshape(n_expert, n_dp, ex_local, 128), axis=1)
    d_combine = finish(routes_t, combine.T.astype(f32), returned.reshape(experts, 128))
    return d_w_down, d_combine.T


def solution(mesh):
    placed = (
        P(("groups", "expert", "dp"), None),
        P(("groups", "expert", "dp"), None),
        P(("groups", "expert", "dp"), None, None),
        P(("groups", "expert", "dp"), None),
        P("expert", "dp", None),
    )
    return jax.shard_map(
        body,
        mesh=mesh,
        in_specs=placed,
        out_specs=(P(("groups", "expert"), "dp", None), P(("groups", "expert", "dp"), None)),
        check_vma=False,
    )
```

```python
import functools

import jax
import jax.numpy as jnp
from jax import lax
from jax.experimental import pallas as pl
from jax.experimental.pallas import tpu as pltpu
from jax.sharding import PartitionSpec as P

MOST = 18
SUPER = 8
TILES = 9
GROUP = ("expert", "dp")
f32, bf16, i32 = jnp.float32, jnp.bfloat16, jnp.int32


def dot(a, b, dims=((1,), (0,))):
    return lax.dot_general(a, b, (dims, ((), ())), preferred_element_type=f32)


def iota(shape, dim):
    return lax.broadcasted_iota(i32, shape, dim)


def params(megabytes):
    return pltpu.CompilerParams(vmem_limit_bytes=megabytes * 2**20)


def cost(flops, nbytes):
    return pl.CostEstimate(flops=int(flops), bytes_accessed=int(nbytes), transcendentals=0)


def token_slots(routes_t, experts):
    top_k, tok = routes_t.shape
    numbers = iota((experts, tok), 0)
    named = jnp.zeros((experts, tok), f32)
    for k in range(top_k):
        named += jnp.where(routes_t[k : k + 1, :] == numbers, 1.0, 0.0)
    before = jnp.where(iota((tok, tok), 0) < iota((tok, tok), 1), 1.0, 0.0)
    return named, dot(named.astype(bf16), before.astype(bf16))


def pack_kernel(n_dp, half, routes_t, routes_flat, weights_flat, hidden, out, target):
    ex = pl.program_id(0)
    experts = pl.num_programs(0) * 2 * half // MOST
    n_routes = routes_flat.shape[1]
    top_k, tok = routes_t.shape
    units = hidden.shape[1]
    part = units // n_dp

    @pl.when(ex == 0)
    def _():
        _, slots = token_slots(routes_t[...], experts)
        shape = (tok, n_routes)
        spread = jnp.where(iota(shape, 1) // top_k == iota(shape, 0), 1.0, 0.0)
        slots = dot(slots.astype(bf16), spread.astype(bf16))
        numbers = iota((experts, n_routes), 0)
        rows = slots + (numbers * MOST).astype(f32)
        rows = jnp.where(routes_flat[...] == numbers, rows, 0.0)
        target[...] = jnp.sum(rows, axis=0, keepdims=True).astype(i32)

    weights = weights_flat[...].astype(f32)
    for side in range(2):
        first = ex * 2 * half + side * half
        chosen = target[...] - first == iota((half, n_routes), 0)
        chosen = jnp.where(chosen, weights, 0.0).astype(bf16)
        rows = dot(chosen, hidden[...]).astype(bf16)
        for d in range(n_dp):
            out[d, :, side * part : (side + 1) * part] = rows[:, d * part : (d + 1) * part]


def pack(routes_t, routes_flat, weights_flat, hidden, n_expert, n_dp, half):
    n_routes, units = hidden.shape
    part = units // n_dp
    whole = lambda shape: pl.BlockSpec(shape, lambda i: (0,) * len(shape))
    return pl.pallas_call(
        functools.partial(pack_kernel, n_dp, half),
        grid=(n_expert,),
        in_specs=[
            whole(routes_t.shape),
            whole(routes_flat.shape),
            whole(weights_flat.shape),
            whole(hidden.shape),
        ],
        out_specs=pl.BlockSpec((n_dp, half, 2 * part), lambda i: (i, 0, 0)),
        out_shape=jax.ShapeDtypeStruct((n_expert * n_dp, half, 2 * part), bf16),
        scratch_shapes=[pltpu.VMEM((1, n_routes), i32)],
        compiler_params=params(56),
        cost_estimate=cost(4 * n_expert * half * n_routes * units, 6 * n_routes * units),
    )(routes_t, routes_flat, weights_flat, hidden)


def tile_rows(i, rows):
    first = min(16 * i // MOST, SUPER - 2)
    place = 16 * i + iota((rows, 1), 0) % 16
    second = place >= MOST * (first + 1)
    slot = place - MOST * first - jnp.where(second, MOST, 0)
    return first, second, slot


def gather_kernel(ex_local, order, routes_t, *refs):
    grads, (weights, out, backs, held) = refs[:SUPER], refs[SUPER:]
    tok = routes_t.shape[2]
    width = held.shape[2]
    rows = 16 * ex_local
    start = pl.program_id(0) * SUPER
    expert = pl.program_id(1)

    @pl.when(expert == 0)
    def _():
        slots = []
        for b in range(SUPER):
            named, before = token_slots(routes_t[order[start + b]], ex_local)
            slots.append(jnp.where(named > 0, before, -1.0))
        shape = (rows, ex_local)
        spread = jnp.where(iota(shape, 0) // 16 == iota(shape, 1), 1.0, 0.0).astype(bf16)
        step = min(512, width)
        for i in range(TILES):
            first, second, slot = tile_rows(i, rows)
            pair = jnp.concatenate([slots[first], slots[first + 1]], axis=1)
            pair = dot(spread, pair.astype(bf16))
            slot = slot.astype(f32)
            wanted = jnp.where(
                iota((rows, 2 * tok), 1) < tok,
                jnp.where(second, -5.0, slot),
                jnp.where(second, slot, -5.0),
            )
            chosen = jnp.where(pair == wanted, 1.0, 0.0).astype(bf16)
            for c in range(0, width, step):
                here = slice(c, c + step)
                both = [grads[first][:, here], grads[first + 1][:, here]]
                found = dot(chosen, jnp.concatenate(both, axis=0))
                found = found.astype(bf16).reshape(ex_local, 16, step)
                held[:, 16 * i : 16 * i + 16, here] = found

    mine = held[expert]
    out[0] = mine
    backs[0] = dot(mine, weights[0], ((1,), (1,)))


def gather(order, routes_t, grads, weights):
    blocks, top_k, tok = routes_t.shape
    ex_local, part, width = weights.shape
    if len(grads) == 1:
        supers, grads = blocks // SUPER, list(grads) * SUPER
    else:
        supers = 1
    rows = supers * SUPER * MOST
    place = lambda j: (lambda s, e, order: (SUPER * s + j if supers > 1 else 0, 0))
    return pl.pallas_call(
        functools.partial(gather_kernel, ex_local),
        grid_spec=pltpu.PrefetchScalarGridSpec(
            num_scalar_prefetch=1,
            grid=(supers, ex_local),
            in_specs=[pl.BlockSpec((blocks, top_k, tok), lambda s, e, order: (0, 0, 0))]
            + [pl.BlockSpec((tok, width), place(j)) for j in range(SUPER)]
            + [pl.BlockSpec((1, part, width), lambda s, e, order: (e, 0, 0))],
            out_specs=[
                pl.BlockSpec((1, SUPER * MOST, width), lambda s, e, order: (e, s, 0)),
                pl.BlockSpec((1, SUPER * MOST, part), lambda s, e, order: (e, s, 0)),
            ],
            scratch_shapes=[pltpu.VMEM((ex_local, SUPER * MOST, width), bf16)],
        ),
        out_shape=[
            jax.ShapeDtypeStruct((ex_local, rows, width), bf16),
            jax.ShapeDtypeStruct((ex_local, rows, part), f32),
        ],
        compiler_params=params(56),
        cost_estimate=cost(
            2 * ex_local * rows * width * (2 * tok + part),
            2 * width * (supers * SUPER * tok + ex_local * (rows + part)),
        ),
    )(order, routes_t, *grads, weights)


def arrange_kernel(ex_local, pieces, order, received, *refs):
    backs, outs, sums = refs[:pieces], refs[pieces : 2 * pieces], refs[2 * pieces]
    _, half, double = received.shape
    part = double // 2
    paired = ex_local % 2 == 0
    some = ex_local // 2 if paired else ex_local
    rows = 16 * some
    lane = iota((rows, 128), 1)
    expert = iota((rows, 1), 0) // 16
    for piece in range(pieces):
        start = (pl.program_id(0) * pieces + piece) * SUPER
        totals = {}
        for i in range(TILES):
            first, second, slot = tile_rows(i, rows)
            block = jnp.where(second, half, 0)
            source = [received[order[start + first]], received[order[start + first + 1]]]
            source = jnp.concatenate(source, axis=0)
            results = []
            for side in range(1 if paired else 2):
                place = expert * MOST + slot - side * half
                inside = (place >= 0) & (place < half)
                column = jnp.where(inside, block + place, -1)
                chosen = iota((rows, 2 * half), 1) == column
                results.append(dot(jnp.where(chosen, 1.0, 0.0).astype(bf16), source))
            if paired:
                sides = [results[0][:, :part], results[0][:, part:]]
            else:
                sides = [results[0][:, :part] + results[1][:, part:]]
            for s, found in enumerate(sides):
                here = slice(s * some, (s + 1) * some)
                tile = slice(16 * i, 16 * i + 16)
                outs[piece][here, tile, :] = found.astype(bf16).reshape(some, 16, part)
                near = backs[piece][here, tile, :].reshape(rows, part)
                total = jnp.sum(found * near, axis=1, keepdims=True)
                total = jnp.where(lane == slot, total, 0.0)
                for b in range(2):
                    mine = jnp.where(second == (b == 1), total, 0.0)
                    mine = jnp.sum(mine.reshape(some, 16, 128), axis=1)
                    key = (first + b, s)
                    totals[key] = totals[key] + mine if key in totals else mine
        for (b, s), total in totals.items():
            sums[order[start + b], s * some : (s + 1) * some, :] = total


def arrange(order, received, backs):
    blocks, half, double = received.shape
    ex_local, rows, part = backs[0].shape
    pieces = len(backs)
    steps = blocks // (SUPER * pieces)
    tall = (ex_local, SUPER * MOST, part)
    return pl.pallas_call(
        functools.partial(arrange_kernel, ex_local, pieces),
        grid_spec=pltpu.PrefetchScalarGridSpec(
            num_scalar_prefetch=1,
            grid=(steps,),
            in_specs=[pl.BlockSpec(received.shape, lambda s, order: (0, 0, 0))]
            + [pl.BlockSpec(tall, lambda s, order: (0, s, 0))] * pieces,
            out_specs=[pl.BlockSpec(tall, lambda s, order: (0, s, 0))] * pieces
            + [pl.BlockSpec((blocks, ex_local, 128), lambda s, order: (0, 0, 0))],
        ),
        out_shape=[jax.ShapeDtypeStruct((ex_local, rows, part), bf16)] * pieces
        + [jax.ShapeDtypeStruct((blocks, ex_local, 128), f32)],
        compiler_params=params(56),
        cost_estimate=cost(
            4 * pieces * ex_local * rows * half * double, pieces * ex_local * rows * part * 8
        ),
    )(order, received, *backs)


def outer_kernel(pieces, *refs):
    hidden, grads, out = refs[:pieces], refs[pieces : 2 * pieces], refs[2 * pieces]
    found = sum(dot(h[0], g[0], ((0,), (0,))) for h, g in zip(hidden, grads))
    if len(refs) == 2 * pieces + 1:
        out[0] = found.astype(bf16)
        return
    total, chunk = refs[-1], pl.program_id(1)

    @pl.when(chunk == 0)
    def _():
        total[...] = found

    @pl.when(chunk > 0)
    def _():
        total[...] += found

    @pl.when(chunk == pl.num_programs(1) - 1)
    def _():
        out[0] = total[...].astype(bf16)


def outer(hidden, grads):
    pieces = len(hidden)
    ex_local, rows, part = hidden[0].shape
    width = grads[0].shape[2]
    chunk = min(rows, 16 * MOST)
    return pl.pallas_call(
        functools.partial(outer_kernel, pieces),
        grid=(ex_local, rows // chunk),
        in_specs=[pl.BlockSpec((1, chunk, part), lambda e, c: (e, c, 0))] * pieces
        + [pl.BlockSpec((1, chunk, width), lambda e, c: (e, c, 0))] * pieces,
        out_specs=pl.BlockSpec((1, part, width), lambda e, c: (e, 0, 0)),
        out_shape=jax.ShapeDtypeStruct((ex_local, part, width), bf16),
        scratch_shapes=[] if rows == chunk else [pltpu.VMEM((part, width), f32)],
        compiler_params=params(56),
        cost_estimate=cost(
            2 * pieces * ex_local * rows * width * part,
            2 * ex_local * (pieces * rows + part) * width,
        ),
    )(*hidden, *grads)


def finish_kernel(routes_t, weights_t, sums, out):
    experts = sums.shape[0]
    top_k, tok = routes_t.shape
    _, slots = token_slots(routes_t[...], experts)
    slots = slots.astype(i32)
    found = jnp.zeros((experts, tok), f32)
    for m in range(MOST):
        found = jnp.where(slots == m, sums[:, m : m + 1], found)
    numbers = iota((experts, tok), 0)
    for k in range(top_k):
        mine = jnp.where(routes_t[k : k + 1, :] == numbers, found, 0.0)
        total = jnp.sum(mine, axis=0, keepdims=True)
        out[k : k + 1, :] = total / weights_t[k : k + 1, :]


def finish(routes_t, weights_t, sums):
    return pl.pallas_call(
        finish_kernel,
        out_shape=jax.ShapeDtypeStruct(routes_t.shape, f32),
        cost_estimate=cost(10000, 100000),
    )(routes_t, weights_t, sums)


def hop(block, axis, flip):
    size = lax.axis_size(axis)
    return lax.ppermute(block, axis, [(i, i ^ flip) for i in range(size)])


def gather_blocks(own, n_expert, n_dp):
    if (n_expert, n_dp) != (4, 4):
        return [[lax.all_gather(own, GROUP, axis=0, tiled=True)]]
    far = hop(own, "expert", 2)
    near = hop(own, "expert", 1)
    side = hop(own, "dp", 2)
    both = hop(far, "expert", 1)
    far_side = hop(far, "dp", 2)
    near_side = hop(near, "dp", 2)
    both_side = hop(both, "dp", 2)
    early = [(0, own), (8, far), (4, near), (2, side)]
    late = [(12, both), (10, far_side), (6, near_side), (14, both_side)]
    twin = lambda some: some + [(index + 1, hop(block, "dp", 1)) for index, block in some]
    return [twin(early), twin(late)]


def body(routes, combine, hidden, d_out, w_down):
    n_expert = lax.axis_size("expert")
    n_dp = lax.axis_size("dp")
    ex_local = w_down.shape[0]
    experts = n_expert * ex_local
    tok, top_k = routes.shape
    blocks = n_expert * n_dp
    half = ex_local * MOST // 2
    routes_t = routes.T
    n_routes = tok * top_k
    grads = gather_blocks(d_out, n_expert, n_dp)
    me = lax.axis_index("expert") * n_dp + lax.axis_index("dp")
    mine = jnp.broadcast_to(routes_t[None], (blocks, top_k, tok))
    all_routes = lax.all_to_all(mine, GROUP, split_axis=0, concat_axis=0, tiled=True)
    all_routes = all_routes - lax.axis_index("expert") * ex_local
    sent = pack(
        routes_t,
        routes.reshape(1, n_routes),
        combine.reshape(1, n_routes),
        hidden.reshape(n_routes, hidden.shape[2]),
        n_expert,
        n_dp,
        half,
    )
    received = lax.all_to_all(sent, GROUP, split_axis=0, concat_axis=0, tiled=True)
    if len(grads) == 1:
        order = [jnp.arange(blocks, dtype=i32)]
    else:
        order = [me ^ jnp.asarray([far for far, _ in some], i32) for some in grads]
        grads = [[block for _, block in some] for some in grads]
    found = [gather(o, all_routes, some, w_down) for o, some in zip(order, grads)]
    order = jnp.concatenate(order)
    *arranged, sums = arrange(order, received, [b for _, b in found])
    returned = lax.all_to_all(sums, GROUP, split_axis=0, concat_axis=0, tiled=True)
    d_w_down = outer(arranged, [g for g, _ in found])
    returned = jnp.sum(returned.reshape(n_expert, n_dp, ex_local, 128), axis=1)
    d_combine = finish(routes_t, combine.T.astype(f32), returned.reshape(experts, 128))
    return d_w_down, d_combine.T


def solution(mesh):
    placed = (
        P(("groups", "expert", "dp"), None),
        P(("groups", "expert", "dp"), None),
        P(("groups", "expert", "dp"), None, None),
        P(("groups", "expert", "dp"), None),
        P("expert", "dp", None),
    )
    return jax.shard_map(
        body,
        mesh=mesh,
        in_specs=placed,
        out_specs=(P(("groups", "expert"), "dp", None), P(("groups", "expert", "dp"), None)),
        check_vma=False,
    )
```

```python
import functools

import jax
import jax.numpy as jnp
from jax import lax
from jax.experimental import pallas as pl
from jax.experimental.pallas import tpu as pltpu
import numpy as np
from jax.sharding import PartitionSpec as P

MOST = 18
SUPER = 8
TILES = 9
GROUP = ("expert", "dp")
f32, bf16, i32 = jnp.float32, jnp.bfloat16, jnp.int32


SMEM = pl.BlockSpec(memory_space=pltpu.SMEM)
VMEM = pl.BlockSpec(memory_space=pltpu.VMEM)


def dot(a, b, dims=((1,), (0,))):
    return lax.dot_general(a, b, (dims, ((), ())), preferred_element_type=f32)


def iota(shape, dim):
    return lax.broadcasted_iota(i32, shape, dim)


def params(megabytes):
    return pltpu.CompilerParams(vmem_limit_bytes=megabytes * 2**20)


def cost(flops, nbytes):
    return pl.CostEstimate(flops=int(flops), bytes_accessed=int(nbytes), transcendentals=0)


def token_slots(routes_t, experts):
    top_k, tok = routes_t.shape
    numbers = iota((experts, tok), 0)
    named = jnp.zeros((experts, tok), f32)
    for k in range(top_k):
        named += jnp.where(routes_t[k : k + 1, :] == numbers, 1.0, 0.0)
    before = jnp.where(iota((tok, tok), 0) < iota((tok, tok), 1), 1.0, 0.0)
    return named, dot(named.astype(bf16), before.astype(bf16))


def pack_kernel(n_dp, half, routes_t, routes_flat, weights_flat, hidden, early, out, copies, target):
    del early
    ex = pl.program_id(0)
    experts = pl.num_programs(0) * 2 * half // MOST
    n_routes = routes_flat.shape[1]
    top_k, tok = routes_t.shape
    part = hidden.shape[1] // n_dp
    copies[...] = jnp.broadcast_to(routes_t[...][None], copies.shape)

    @pl.when(ex == 0)
    def _():
        _, slots = token_slots(routes_t[...], experts)
        shape = (tok, n_routes)
        spread = jnp.where(iota(shape, 1) // top_k == iota(shape, 0), 1.0, 0.0)
        slots = dot(slots.astype(bf16), spread.astype(bf16))
        numbers = iota((experts, n_routes), 0)
        rows = slots + (numbers * MOST).astype(f32)
        rows = jnp.where(routes_flat[...] == numbers, rows, 0.0)
        target[...] = jnp.sum(rows, axis=0, keepdims=True).astype(i32)

    weights = weights_flat[...].astype(f32)
    for side in range(2):
        first = ex * 2 * half + side * half
        chosen = target[...] - first == iota((half, n_routes), 0)
        chosen = jnp.where(chosen, weights, 0.0).astype(bf16)
        rows = dot(chosen, hidden[...]).astype(bf16)
        for d in range(n_dp):
            out[d, :, side * part : (side + 1) * part] = rows[:, d * part : (d + 1) * part]


def pack(routes_t, routes_flat, weights_flat, hidden, early, n_expert, n_dp, half):
    n_routes, units = hidden.shape
    part = units // n_dp
    whole = lambda shape: pl.BlockSpec(shape, lambda i: (0,) * len(shape))
    return pl.pallas_call(
        functools.partial(pack_kernel, n_dp, half),
        grid=(n_expert,),
        in_specs=[
            whole(routes_t.shape),
            whole(routes_flat.shape),
            whole(weights_flat.shape),
            whole(hidden.shape),
            pl.BlockSpec(memory_space=pl.ANY),
        ],
        out_specs=[
            pl.BlockSpec((n_dp, half, 2 * part), lambda i: (i, 0, 0)),
            pl.BlockSpec((n_dp,) + routes_t.shape, lambda i: (i, 0, 0)),
        ],
        out_shape=[
            jax.ShapeDtypeStruct((n_expert * n_dp, half, 2 * part), bf16),
            jax.ShapeDtypeStruct((n_expert * n_dp,) + routes_t.shape, i32),
        ],
        scratch_shapes=[pltpu.VMEM((1, n_routes), i32)],
        compiler_params=params(16),
        cost_estimate=cost(4 * n_expert * half * n_routes * units, 6 * n_routes * units),
    )(routes_t, routes_flat, weights_flat, hidden, early)


def after_kernel(*refs):
    pass


def after(array, *events):
    anywhere = pl.BlockSpec(memory_space=pl.ANY)
    return pl.pallas_call(
        after_kernel,
        in_specs=[anywhere] * (1 + len(events)),
        out_specs=anywhere,
        out_shape=jax.ShapeDtypeStruct(array.shape, array.dtype),
        input_output_aliases={0: 0},
    )(array, *events)


def tile_rows(i, rows):
    first = min(16 * i // MOST, SUPER - 2)
    place = 16 * i + iota((rows, 1), 0) % 16
    second = place >= MOST * (first + 1)
    slot = place - MOST * first - jnp.where(second, MOST, 0)
    return first, second, slot


def block_at(place, order, index):
    return place[0] ^ order[index] if order else pl.program_id(0) * SUPER + index


def gather_rows(order, place, routes_t, grads, out, start=0):
    tok = routes_t.shape[2]
    ex_local, _, width = out.shape
    rows = 16 * ex_local
    slots = []
    for b in range(SUPER):
        mine = routes_t[block_at(place, order, b)] - place[1]
        named, before = token_slots(mine, ex_local)
        slots.append(jnp.where(named > 0, before, -1.0))
    shape = (rows, ex_local)
    spread = jnp.where(iota(shape, 0) // 16 == iota(shape, 1), 1.0, 0.0).astype(bf16)
    step = min(512, width)
    for i in range(TILES):
        first, second, slot = tile_rows(i, rows)
        pair = jnp.concatenate([slots[first], slots[first + 1]], axis=1)
        pair = dot(spread, pair.astype(bf16))
        slot = slot.astype(f32)
        wanted = jnp.where(
            iota((rows, 2 * tok), 1) < tok,
            jnp.where(second, -5.0, slot),
            jnp.where(second, slot, -5.0),
        )
        chosen = jnp.where(pair == wanted, 1.0, 0.0).astype(bf16)
        near, far = grads(first), grads(first + 1)
        tile = start + 16 * i
        for c in range(0, width, step):
            here = slice(c, c + step)
            both = jnp.concatenate([near[:, here], far[:, here]], axis=0)
            found = dot(chosen, both).astype(bf16).reshape(ex_local, 16, step)
            out[:, tile : tile + 16, here] = found


def gather_kernel(place, routes_t, *refs):
    gather_rows(None, place, routes_t, lambda b: refs[b], refs[SUPER])


def gather(place, routes_t, grads, ex_local):
    blocks, top_k, tok = routes_t.shape
    width = grads.shape[1]
    tall = SUPER * MOST
    picked = lambda j: pl.BlockSpec((tok, width), lambda s: (SUPER * s + j, 0))
    return pl.pallas_call(
        gather_kernel,
        grid=(blocks // SUPER,),
        in_specs=[SMEM, pl.BlockSpec(routes_t.shape, lambda s: (0, 0, 0))]
        + [picked(j) for j in range(SUPER)],
        out_specs=pl.BlockSpec((ex_local, tall, width), lambda s: (0, s, 0)),
        out_shape=jax.ShapeDtypeStruct((ex_local, blocks * MOST, width), bf16),
        compiler_params=params(48),
    )(place, routes_t, *([grads] * SUPER))


def fetch(sources, held, sems):
    copies = [
        pltpu.make_async_copy(source, held.at[i], sems.at[i]) for i, source in enumerate(sources)
    ]
    for copy in copies:
        copy.start()
    waited = set()

    def block(i):
        if i not in waited:
            copies[i].wait()
            waited.add(i)
        return held.at[i]

    return block


def arrange_kernel(orders, ex_local, place, received, out):
    _, half, double = received.shape
    part = double // 2
    paired = ex_local % 2 == 0
    some = ex_local // 2 if paired else ex_local
    rows = 16 * some
    expert = iota((rows, 1), 0) // 16
    for i in range(TILES):
        first, second, slot = tile_rows(i, rows)
        block = jnp.where(second, half, 0)
        chosen = []
        for side in range(1 if paired else 2):
            spot = expert * MOST + slot - side * half
            column = jnp.where((spot >= 0) & (spot < half), block + spot, -1)
            hit = iota((rows, 2 * half), 1) == column
            chosen.append(jnp.where(hit, 1.0, 0.0).astype(bf16))
        for piece, order in enumerate(orders):
            pair = [received[block_at(place, order, first + b)] for b in range(2)]
            pair = jnp.concatenate(pair, axis=0)
            results = [dot(c, pair) for c in chosen]
            if paired:
                sides = [results[0][:, :part], results[0][:, part:]]
            else:
                sides = [results[0][:, :part] + results[1][:, part:]]
            tile = piece * SUPER * MOST + 16 * i
            for s, found in enumerate(sides):
                here = slice(s * some, (s + 1) * some)
                out[here, tile : tile + 16, :] = found.astype(bf16).reshape(some, 16, part)


def arrange(place, orders, received, ex_local):
    blocks, half, double = received.shape
    part = double // 2
    shape = (ex_local, blocks * MOST, part)
    kernel = functools.partial(arrange_kernel, orders, ex_local)
    if orders[0]:
        return pl.pallas_call(
            kernel,
            in_specs=[SMEM, VMEM],
            out_specs=VMEM,
            out_shape=jax.ShapeDtypeStruct(shape, bf16),
            compiler_params=params(24),
            cost_estimate=cost(4 * ex_local * blocks * MOST * half * double, 2**22),
        )(place, received)
    return pl.pallas_call(
        kernel,
        grid=(blocks // SUPER,),
        in_specs=[SMEM, pl.BlockSpec(received.shape, lambda s: (0, 0, 0))],
        out_specs=pl.BlockSpec((ex_local, SUPER * MOST, part), lambda s: (0, s, 0)),
        out_shape=jax.ShapeDtypeStruct(shape, bf16),
        compiler_params=params(32),
    )(place, received)


def back_rows(place, expert, hidden, grads, weights, sums):
    found = dot(grads, weights, ((1,), (1,)))
    total = jnp.sum(hidden.astype(f32) * found, axis=1, keepdims=True)
    sums[...] += jnp.where(iota(sums.shape, 1) == place[1] + expert, total, 0.0)


def back_kernel(place, hidden, grads, weights, out, sums):
    expert = pl.program_id(1)

    @pl.when(expert == 0)
    def _():
        sums[...] = jnp.zeros_like(sums)

    back_rows(place, expert, hidden[0], grads[0], weights[0], sums)

    @pl.when(expert == pl.num_programs(1) - 1)
    def _():
        for b in range(SUPER):
            out[b] = sums[b * MOST : (b + 1) * MOST, :]


def back(place, hidden, grads, weights):
    ex_local, rows, width = grads.shape
    part = weights.shape[1]
    tall = SUPER * MOST
    return pl.pallas_call(
        back_kernel,
        grid=(rows // tall, ex_local),
        in_specs=[
            SMEM,
            pl.BlockSpec((1, tall, part), lambda s, e: (e, s, 0)),
            pl.BlockSpec((1, tall, width), lambda s, e: (e, s, 0)),
            pl.BlockSpec((1, part, width), lambda s, e: (e, 0, 0)),
        ],
        out_specs=pl.BlockSpec((SUPER, MOST, 128), lambda s, e: (s, 0, 0)),
        out_shape=jax.ShapeDtypeStruct((rows // MOST, MOST, 128), f32),
        scratch_shapes=[pltpu.VMEM((tall, 128), f32)],
        compiler_params=params(32),
    )(place, hidden, grads, weights)


def gather_back_kernel(orders, place, routes_t, hidden, weights, *refs):
    piece = len(orders) - 1
    blocks, refs = refs[:SUPER], refs[SUPER:]
    earlier, (out, sums, held, rows, sems) = refs[:piece], refs[piece:]
    step = pl.program_id(0)

    @pl.when(step == 0)
    def _():
        sums[...] = jnp.zeros_like(sums)
        gather_rows(orders[-1], place, routes_t, fetch(blocks, held, sems), rows)

    for j in range(GROUPED):
        expert = step * GROUPED + j
        back_rows(place, expert, hidden[j], rows[expert], weights[j], sums)

    @pl.when(step == pl.num_programs(0) - 1)
    def _():
        for b in range(SUPER):
            mine = sums[b * MOST : (b + 1) * MOST, :]
            if earlier:
                out[block_at(place, orders[0], b)] = earlier[0][b]
                out[block_at(place, orders[1], b)] = mine
            else:
                out[b] = mine


def gather_back(place, orders, routes_t, hidden, weights, blocks, earlier):
    ex_local, part, width = weights.shape
    tok = blocks[0].shape[0]
    piece = len(orders) - 1
    tall = SUPER * MOST
    return pl.pallas_call(
        functools.partial(gather_back_kernel, orders),
        grid=(ex_local // GROUPED,),
        in_specs=[
            SMEM,
            VMEM,
            pl.BlockSpec((GROUPED, tall, part), lambda e: (e, piece, 0)),
            pl.BlockSpec((GROUPED, part, width), lambda e: (e, 0, 0)),
        ]
        + [pl.BlockSpec(memory_space=pl.ANY)] * SUPER
        + [VMEM] * len(earlier),
        out_specs=pl.BlockSpec((SUPER * (piece + 1), MOST, 128), lambda e: (0, 0, 0)),
        out_shape=jax.ShapeDtypeStruct((SUPER * (piece + 1), MOST, 128), f32),
        scratch_shapes=[
            pltpu.VMEM((tall, 128), f32),
            pltpu.VMEM((SUPER, tok, width), bf16),
            pltpu.VMEM((ex_local, tall, width), bf16),
            pltpu.SemaphoreType.DMA((SUPER,)),
        ],
        compiler_params=params(40),
        cost_estimate=cost(
            2 * ex_local * tall * width * (part + 2 * tok), 2 * ex_local * part * width
        ),
    )(place, routes_t, hidden, weights, *blocks, *earlier)


GROUPED = 2


def gather_outer_kernel(orders, place, routes_t, hidden, *refs):
    count = SUPER * len(orders)
    blocks, (out, held, rows, sems) = refs[:count], refs[count:]
    step = pl.program_id(0)
    width = out.shape[2]
    columns = min(512, width)

    @pl.when(step == 0)
    def _():
        block = fetch(blocks, held, sems)
        for piece, order in enumerate(orders):
            mine = lambda b, piece=piece: block(piece * SUPER + b)
            gather_rows(order, place, routes_t, mine, rows, piece * SUPER * MOST)

    for j in range(GROUPED):
        expert = step * GROUPED + j
        for c in range(0, width, columns):
            here = slice(c, c + columns)
            found = dot(hidden[j], rows[expert, :, here], ((0,), (0,)))
            out[j, :, here] = found.astype(bf16)


def gather_outer(place, orders, routes_t, hidden, blocks):
    ex_local, tall, part = hidden.shape
    tok, width = blocks[0].shape
    return pl.pallas_call(
        functools.partial(gather_outer_kernel, orders),
        grid=(ex_local // GROUPED,),
        in_specs=[SMEM, VMEM, pl.BlockSpec((GROUPED, tall, part), lambda e: (e, 0, 0))]
        + [pl.BlockSpec(memory_space=pl.ANY)] * len(blocks),
        out_specs=pl.BlockSpec((GROUPED, part, width), lambda e: (e, 0, 0)),
        out_shape=jax.ShapeDtypeStruct((ex_local, part, width), bf16),
        scratch_shapes=[
            pltpu.VMEM((len(blocks), tok, width), bf16),
            pltpu.VMEM((ex_local, tall, width), bf16),
            pltpu.SemaphoreType.DMA((len(blocks),)),
        ],
        compiler_params=params(52),
        cost_estimate=cost(
            2 * ex_local * tall * width * (part + 2 * tok), 2 * ex_local * part * width
        ),
    )(place, routes_t, hidden, *blocks)


def kept(array):
    return pltpu.with_memory_space_constraint(array, pltpu.VMEM)


def outer_kernel(hidden, grads, out, total):
    chunk = pl.program_id(1)

    @pl.when(chunk == 0)
    def _():
        total[...] = jnp.zeros_like(total)

    total[...] += dot(hidden[0], grads[0], ((0,), (0,)))

    @pl.when(chunk == pl.num_programs(1) - 1)
    def _():
        out[0] = total[...].astype(bf16)


def outer(hidden, grads):
    ex_local, rows, part = hidden.shape
    width = grads.shape[2]
    tall = SUPER * MOST
    return pl.pallas_call(
        outer_kernel,
        grid=(ex_local, rows // tall),
        in_specs=[
            pl.BlockSpec((1, tall, part), lambda e, c: (e, c, 0)),
            pl.BlockSpec((1, tall, width), lambda e, c: (e, c, 0)),
        ],
        out_specs=pl.BlockSpec((1, part, width), lambda e, c: (e, 0, 0)),
        out_shape=jax.ShapeDtypeStruct((ex_local, part, width), bf16),
        scratch_shapes=[pltpu.VMEM((part, width), f32)],
        compiler_params=params(32),
    )(hidden, grads)


def finish_kernel(experts, routes_t, weights_t, returned, out):
    top_k, tok = routes_t.shape
    total = jnp.sum(returned[...], axis=0)
    total = jnp.concatenate([total, jnp.zeros((128 - MOST, 128), f32)], axis=0)
    total = total.T[:experts]
    _, slots = token_slots(routes_t[...], experts)
    slots = slots.astype(i32)
    found = jnp.zeros((experts, tok), f32)
    for m in range(MOST):
        found = jnp.where(slots == m, total[:, m : m + 1], found)
    numbers = iota((experts, tok), 0)
    for k in range(top_k):
        mine = jnp.where(routes_t[k : k + 1, :] == numbers, found, 0.0)
        mine = jnp.sum(mine, axis=0, keepdims=True)
        out[k : k + 1, :] = mine / weights_t[k : k + 1, :].astype(f32)


def finish(routes_t, weights_t, returned, experts):
    return pl.pallas_call(
        functools.partial(finish_kernel, experts),
        out_shape=jax.ShapeDtypeStruct(routes_t.shape, f32),
        compiler_params=params(24),
        cost_estimate=cost(10000, 100000),
    )(routes_t, weights_t, returned)


def hop(block, axis, flip):
    size = lax.axis_size(axis)
    return lax.ppermute(block, axis, [(i, i ^ flip) for i in range(size)])


def body(routes, combine, hidden, d_out, w_down):
    n_expert = lax.axis_size("expert")
    n_dp = lax.axis_size("dp")
    ex_local = w_down.shape[0]
    experts = n_expert * ex_local
    tok, top_k = routes.shape
    half = ex_local * MOST // 2
    routes_t, weights_t = routes.T, combine.T
    n_routes = tok * top_k
    me, mine = lax.axis_index("expert") * n_dp + lax.axis_index("dp"), lax.axis_index("expert")
    place = jnp.stack([me, mine * ex_local]).astype(i32)
    small = (n_expert, n_dp) == (4, 4)
    trade = lambda x: lax.all_to_all(x, GROUP, split_axis=0, concat_axis=0, tiled=True)
    if small:
        near = hop(d_out, "expert", 1)
        side = hop(d_out, "dp", 2)
        far = hop(d_out, "expert", 2)
        twin = hop(d_out, "dp", 1)
    else:
        twin = d_out
    sent, copies = pack(
        routes_t,
        routes.reshape(1, n_routes),
        combine.reshape(1, n_routes),
        hidden.reshape(n_routes, hidden.shape[2]),
        twin,
        n_expert,
        n_dp,
        half,
    )
    all_routes = trade(copies)
    if small:
        received = trade(after(sent, near, side, far))
        near_side = hop(near, "dp", 2)
        far_side = hop(far, "dp", 2)
        both = hop(far, "expert", 1)
        both_side = hop(both, "dp", 2)
        early = [(0, d_out), (4, near), (2, side), (8, far)]
        late = [(6, near_side), (10, far_side), (12, both), (14, both_side)]
        early = early + [(1, twin)] + [(n + 1, hop(x, "dp", 1)) for n, x in early[1:]]
        late = late + [(n + 1, hop(x, "dp", 1)) for n, x in late]
        orders = [[n for n, _ in some] for some in (early, late)]
        blocks = [[x for _, x in some] for some in (early, late)]
        arranged = arrange(place, orders, received, ex_local)
        sums = []
        for i, some in enumerate(blocks):
            now = orders[: i + 1]
            sums = [gather_back(place, now, all_routes, arranged, w_down, some, sums)]
        sums = sums[0]
        d_w_down = gather_outer(place, orders, all_routes, arranged, sum(blocks, []))
    else:
        received = trade(sent)
        grads = lax.all_gather(d_out, GROUP, axis=0, tiled=True)
        grads = gather(place, all_routes, grads, ex_local)
        arranged = arrange(place, [None], received, ex_local)
        sums = back(place, arranged, grads, w_down)
        d_w_down = outer(arranged, grads)
    d_combine = finish(routes_t, weights_t, trade(sums), experts)
    return d_w_down, d_combine.T


def solution(mesh):
    placed = (
        P(("groups", "expert", "dp"), None),
        P(("groups", "expert", "dp"), None),
        P(("groups", "expert", "dp"), None, None),
        P(("groups", "expert", "dp"), None),
        P("expert", "dp", None),
    )
    return jax.shard_map(
        body,
        mesh=mesh,
        in_specs=placed,
        out_specs=(P(("groups", "expert"), "dp", None), P(("groups", "expert", "dp"), None)),
        check_vma=False,
    )
```

```python
import functools

import jax
import jax.numpy as jnp
from jax import lax
from jax.experimental import pallas as pl
from jax.experimental.pallas import tpu as pltpu
import numpy as np
from jax.sharding import PartitionSpec as P

MOST = 18
SUPER = 8
TILES = 9
GROUP = ("expert", "dp")
f32, bf16, i32 = jnp.float32, jnp.bfloat16, jnp.int32


SMEM = pl.BlockSpec(memory_space=pltpu.SMEM)
VMEM = pl.BlockSpec(memory_space=pltpu.VMEM)


def dot(a, b, dims=((1,), (0,))):
    return lax.dot_general(a, b, (dims, ((), ())), preferred_element_type=f32)


def iota(shape, dim):
    return lax.broadcasted_iota(i32, shape, dim)


def params(megabytes):
    return pltpu.CompilerParams(vmem_limit_bytes=megabytes * 2**20)


def cost(flops, nbytes):
    return pl.CostEstimate(flops=int(flops), bytes_accessed=int(nbytes), transcendentals=0)


def token_slots(routes_t, experts):
    top_k, tok = routes_t.shape
    numbers = iota((experts, tok), 0)
    named = jnp.zeros((experts, tok), f32)
    for k in range(top_k):
        named += jnp.where(routes_t[k : k + 1, :] == numbers, 1.0, 0.0)
    before = jnp.where(iota((tok, tok), 0) < iota((tok, tok), 1), 1.0, 0.0)
    return named, dot(named.astype(bf16), before.astype(bf16))


def pack_kernel(n_dp, half, routes_t, routes_flat, weights_flat, hidden, early, out, copies, target):
    del early
    ex = pl.program_id(0)
    experts = pl.num_programs(0) * 2 * half // MOST
    n_routes = routes_flat.shape[1]
    top_k, tok = routes_t.shape
    part = hidden.shape[1] // n_dp
    copies[...] = jnp.broadcast_to(routes_t[...][None], copies.shape)

    @pl.when(ex == 0)
    def _():
        _, slots = token_slots(routes_t[...], experts)
        shape = (tok, n_routes)
        spread = jnp.where(iota(shape, 1) // top_k == iota(shape, 0), 1.0, 0.0)
        slots = dot(slots.astype(bf16), spread.astype(bf16))
        numbers = iota((experts, n_routes), 0)
        rows = slots + (numbers * MOST).astype(f32)
        rows = jnp.where(routes_flat[...] == numbers, rows, 0.0)
        target[...] = jnp.sum(rows, axis=0, keepdims=True).astype(i32)

    weights = weights_flat[...].astype(f32)
    for side in range(2):
        first = ex * 2 * half + side * half
        chosen = target[...] - first == iota((half, n_routes), 0)
        chosen = jnp.where(chosen, weights, 0.0).astype(bf16)
        rows = dot(chosen, hidden[...]).astype(bf16)
        for d in range(n_dp):
            out[d, :, side * part : (side + 1) * part] = rows[:, d * part : (d + 1) * part]


def pack(routes_t, routes_flat, weights_flat, hidden, early, n_expert, n_dp, half):
    n_routes, units = hidden.shape
    part = units // n_dp
    whole = lambda shape: pl.BlockSpec(shape, lambda i: (0,) * len(shape))
    return pl.pallas_call(
        functools.partial(pack_kernel, n_dp, half),
        grid=(n_expert,),
        in_specs=[
            whole(routes_t.shape),
            whole(routes_flat.shape),
            whole(weights_flat.shape),
            whole(hidden.shape),
            pl.BlockSpec(memory_space=pl.ANY),
        ],
        out_specs=[
            pl.BlockSpec((n_dp, half, 2 * part), lambda i: (i, 0, 0)),
            pl.BlockSpec((n_dp,) + routes_t.shape, lambda i: (i, 0, 0)),
        ],
        out_shape=[
            jax.ShapeDtypeStruct((n_expert * n_dp, half, 2 * part), bf16),
            jax.ShapeDtypeStruct((n_expert * n_dp,) + routes_t.shape, i32),
        ],
        scratch_shapes=[pltpu.VMEM((1, n_routes), i32)],
        compiler_params=params(16),
        cost_estimate=cost(4 * n_expert * half * n_routes * units, 6 * n_routes * units),
    )(routes_t, routes_flat, weights_flat, hidden, early)


def after_kernel(*refs):
    pass


def after(array, *events):
    anywhere = pl.BlockSpec(memory_space=pl.ANY)
    return pl.pallas_call(
        after_kernel,
        in_specs=[anywhere] * (1 + len(events)),
        out_specs=anywhere,
        out_shape=jax.ShapeDtypeStruct(array.shape, array.dtype),
        input_output_aliases={0: 0},
    )(array, *events)


def tile_rows(i, rows):
    first = min(16 * i // MOST, SUPER - 2)
    place = 16 * i + iota((rows, 1), 0) % 16
    second = place >= MOST * (first + 1)
    slot = place - MOST * first - jnp.where(second, MOST, 0)
    return first, second, slot


def block_at(place, order, index):
    return place[0] ^ order[index] if order else pl.program_id(0) * SUPER + index


def gather_rows(order, place, routes_t, grads, out, start=0):
    tok = routes_t.shape[2]
    ex_local, _, width = out.shape
    rows = 16 * ex_local
    slots = []
    for b in range(SUPER):
        mine = routes_t[block_at(place, order, b)] - place[1]
        named, before = token_slots(mine, ex_local)
        slots.append(jnp.where(named > 0, before, -1.0))
    shape = (rows, ex_local)
    spread = jnp.where(iota(shape, 0) // 16 == iota(shape, 1), 1.0, 0.0).astype(bf16)
    step = min(512, width)
    for i in range(TILES):
        first, second, slot = tile_rows(i, rows)
        pair = jnp.concatenate([slots[first], slots[first + 1]], axis=1)
        pair = dot(spread, pair.astype(bf16))
        slot = slot.astype(f32)
        wanted = jnp.where(
            iota((rows, 2 * tok), 1) < tok,
            jnp.where(second, -5.0, slot),
            jnp.where(second, slot, -5.0),
        )
        chosen = jnp.where(pair == wanted, 1.0, 0.0).astype(bf16)
        near, far = grads(first), grads(first + 1)
        tile = start + 16 * i
        for c in range(0, width, step):
            here = slice(c, c + step)
            both = jnp.concatenate([near[:, here], far[:, here]], axis=0)
            found = dot(chosen, both).astype(bf16).reshape(ex_local, 16, step)
            out[:, tile : tile + 16, here] = found


def gather_kernel(place, routes_t, *refs):
    gather_rows(None, place, routes_t, lambda b: refs[b], refs[SUPER])


def gather(place, routes_t, grads, ex_local):
    blocks, top_k, tok = routes_t.shape
    width = grads.shape[1]
    tall = SUPER * MOST
    picked = lambda j: pl.BlockSpec((tok, width), lambda s: (SUPER * s + j, 0))
    return pl.pallas_call(
        gather_kernel,
        grid=(blocks // SUPER,),
        in_specs=[SMEM, pl.BlockSpec(routes_t.shape, lambda s: (0, 0, 0))]
        + [picked(j) for j in range(SUPER)],
        out_specs=pl.BlockSpec((ex_local, tall, width), lambda s: (0, s, 0)),
        out_shape=jax.ShapeDtypeStruct((ex_local, blocks * MOST, width), bf16),
        compiler_params=params(48),
    )(place, routes_t, *([grads] * SUPER))


def fetch(sources, held, sems):
    copies = [
        pltpu.make_async_copy(source, held.at[i], sems.at[i]) for i, source in enumerate(sources)
    ]
    for copy in copies:
        copy.start()
    waited = set()

    def block(i):
        if i not in waited:
            copies[i].wait()
            waited.add(i)
        return held.at[i]

    return block


def arrange_kernel(orders, ex_local, place, received, out):
    _, half, double = received.shape
    part = double // 2
    paired = ex_local % 2 == 0
    some = ex_local // 2 if paired else ex_local
    rows = 16 * some
    expert = iota((rows, 1), 0) // 16
    for i in range(TILES):
        first, second, slot = tile_rows(i, rows)
        block = jnp.where(second, half, 0)
        chosen = []
        for side in range(1 if paired else 2):
            spot = expert * MOST + slot - side * half
            column = jnp.where((spot >= 0) & (spot < half), block + spot, -1)
            hit = iota((rows, 2 * half), 1) == column
            chosen.append(jnp.where(hit, 1.0, 0.0).astype(bf16))
        for piece, order in enumerate(orders):
            pair = [received[block_at(place, order, first + b)] for b in range(2)]
            pair = jnp.concatenate(pair, axis=0)
            results = [dot(c, pair) for c in chosen]
            if paired:
                sides = [results[0][:, :part], results[0][:, part:]]
            else:
                sides = [results[0][:, :part] + results[1][:, part:]]
            tile = piece * SUPER * MOST + 16 * i
            for s, found in enumerate(sides):
                here = slice(s * some, (s + 1) * some)
                out[here, tile : tile + 16, :] = found.astype(bf16).reshape(some, 16, part)


def arrange(place, orders, received, ex_local):
    blocks, half, double = received.shape
    part = double // 2
    shape = (ex_local, blocks * MOST, part)
    kernel = functools.partial(arrange_kernel, orders, ex_local)
    if orders[0]:
        return pl.pallas_call(
            kernel,
            in_specs=[SMEM, VMEM],
            out_specs=VMEM,
            out_shape=jax.ShapeDtypeStruct(shape, bf16),
            compiler_params=params(24),
            cost_estimate=cost(4 * ex_local * blocks * MOST * half * double, 2**22),
        )(place, received)
    return pl.pallas_call(
        kernel,
        grid=(blocks // SUPER,),
        in_specs=[SMEM, pl.BlockSpec(received.shape, lambda s: (0, 0, 0))],
        out_specs=pl.BlockSpec((ex_local, SUPER * MOST, part), lambda s: (0, s, 0)),
        out_shape=jax.ShapeDtypeStruct(shape, bf16),
        compiler_params=params(32),
    )(place, received)


def back_rows(place, expert, hidden, grads, weights, sums):
    found = dot(grads, weights, ((1,), (1,)))
    total = jnp.sum(hidden.astype(f32) * found, axis=1, keepdims=True)
    sums[...] += jnp.where(iota(sums.shape, 1) == place[1] + expert, total, 0.0)


def back_kernel(place, hidden, grads, weights, out, sums):
    expert = pl.program_id(1)

    @pl.when(expert == 0)
    def _():
        sums[...] = jnp.zeros_like(sums)

    back_rows(place, expert, hidden[0], grads[0], weights[0], sums)

    @pl.when(expert == pl.num_programs(1) - 1)
    def _():
        for b in range(SUPER):
            out[b] = sums[b * MOST : (b + 1) * MOST, :]


def back(place, hidden, grads, weights):
    ex_local, rows, width = grads.shape
    part = weights.shape[1]
    tall = SUPER * MOST
    return pl.pallas_call(
        back_kernel,
        grid=(rows // tall, ex_local),
        in_specs=[
            SMEM,
            pl.BlockSpec((1, tall, part), lambda s, e: (e, s, 0)),
            pl.BlockSpec((1, tall, width), lambda s, e: (e, s, 0)),
            pl.BlockSpec((1, part, width), lambda s, e: (e, 0, 0)),
        ],
        out_specs=pl.BlockSpec((SUPER, MOST, 128), lambda s, e: (s, 0, 0)),
        out_shape=jax.ShapeDtypeStruct((rows // MOST, MOST, 128), f32),
        scratch_shapes=[pltpu.VMEM((tall, 128), f32)],
        compiler_params=params(32),
    )(place, hidden, grads, weights)


def early_kernel(order, place, routes_t, weights, *refs):
    blocks, (out, held, rows, sems) = refs[:SUPER], refs[SUPER:]
    step = pl.program_id(0)

    @pl.when(step == 0)
    def _():
        gather_rows(order, place, routes_t, fetch(blocks, held, sems), rows)

    for j in range(GROUPED):
        out[j] = dot(rows[step * GROUPED + j], weights[j], ((1,), (1,)))


def late_kernel(orders, place, routes_t, weights, hidden, backs, *refs):
    blocks, (out, sums, held, rows, sems) = refs[:SUPER], refs[SUPER:]
    step = pl.program_id(0)
    tall, width = rows.shape[1:]
    columns = min(512, width)

    @pl.when(step == 0)
    def _():
        sums[...] = jnp.zeros_like(sums)
        gather_rows(orders[1], place, routes_t, fetch(blocks, held, sems), rows)

    lane = iota((tall, 128), 1) - place[1]
    for j in range(GROUPED):
        expert = step * GROUPED + j
        found = hidden[j, :tall, :].astype(f32) * backs[j]
        total = jnp.sum(found, axis=1, keepdims=True)
        sums[:tall, :] += jnp.where(lane == expert, total, 0.0)
        mine = hidden[j, tall:, :]
        found = jnp.zeros((tall, 128), f32)
        for c in range(0, width, columns):
            here = slice(c, c + columns)
            part = dot(mine, weights[j, :, here]) * rows[expert, :, here].astype(f32)
            for piece in range(0, columns, 128):
                found += part[:, piece : piece + 128]
        total = jnp.sum(found, axis=1, keepdims=True)
        sums[tall:, :] += jnp.where(lane == expert, total, 0.0)

    @pl.when(step == pl.num_programs(0) - 1)
    def _():
        for i, order in enumerate(orders):
            for b in range(SUPER):
                start = (i * SUPER + b) * MOST
                out[block_at(place, order, b)] = sums[start : start + MOST, :]


def gather_back(place, orders, routes_t, weights, blocks, hidden=None, backs=None):
    ex_local, part, width = weights.shape
    tok = blocks[0].shape[0]
    tall = SUPER * MOST
    scratch = [
        pltpu.VMEM((SUPER, tok, width), bf16),
        pltpu.VMEM((ex_local, tall, width), bf16),
        pltpu.SemaphoreType.DMA((SUPER,)),
    ]
    grouped = lambda rows, columns: pl.BlockSpec((GROUPED, rows, columns), lambda e: (e, 0, 0))
    in_specs = [SMEM, VMEM, grouped(part, width)]
    anywhere = [pl.BlockSpec(memory_space=pl.ANY)] * SUPER
    rest = dict(
        grid=(ex_local // GROUPED,),
        compiler_params=params(40),
        cost_estimate=cost(
            2 * ex_local * tall * width * (part + 2 * tok), 2 * ex_local * part * width
        ),
    )
    if hidden is None:
        return pl.pallas_call(
            functools.partial(early_kernel, orders[0]),
            in_specs=in_specs + anywhere,
            out_specs=grouped(tall, part),
            out_shape=jax.ShapeDtypeStruct((ex_local, tall, part), f32),
            scratch_shapes=scratch,
            **rest,
        )(place, routes_t, weights, *blocks)
    count = SUPER * len(orders)
    return pl.pallas_call(
        functools.partial(late_kernel, orders),
        in_specs=in_specs + [grouped(2 * tall, part), grouped(tall, part)] + anywhere,
        out_specs=pl.BlockSpec((count, MOST, 128), lambda e: (0, 0, 0)),
        out_shape=jax.ShapeDtypeStruct((count, MOST, 128), f32),
        scratch_shapes=[pltpu.VMEM((2 * tall, 128), f32)] + scratch,
        **rest,
    )(place, routes_t, weights, hidden, backs, *blocks)


GROUPED = 2


def gather_outer_kernel(orders, place, routes_t, hidden, *refs):
    count = SUPER * len(orders)
    blocks, (out, held, rows, sems) = refs[:count], refs[count:]
    step = pl.program_id(0)
    width = out.shape[2]
    columns = min(512, width)

    @pl.when(step == 0)
    def _():
        block = fetch(blocks, held, sems)
        for piece, order in enumerate(orders):
            mine = lambda b, piece=piece: block(piece * SUPER + b)
            gather_rows(order, place, routes_t, mine, rows, piece * SUPER * MOST)

    for j in range(GROUPED):
        expert = step * GROUPED + j
        for c in range(0, width, columns):
            here = slice(c, c + columns)
            found = dot(hidden[j], rows[expert, :, here], ((0,), (0,)))
            out[j, :, here] = found.astype(bf16)


def gather_outer(place, orders, routes_t, hidden, blocks):
    ex_local, tall, part = hidden.shape
    tok, width = blocks[0].shape
    return pl.pallas_call(
        functools.partial(gather_outer_kernel, orders),
        grid=(ex_local // GROUPED,),
        in_specs=[SMEM, VMEM, pl.BlockSpec((GROUPED, tall, part), lambda e: (e, 0, 0))]
        + [pl.BlockSpec(memory_space=pl.ANY)] * len(blocks),
        out_specs=pl.BlockSpec((GROUPED, part, width), lambda e: (e, 0, 0)),
        out_shape=jax.ShapeDtypeStruct((ex_local, part, width), bf16),
        scratch_shapes=[
            pltpu.VMEM((len(blocks), tok, width), bf16),
            pltpu.VMEM((ex_local, tall, width), bf16),
            pltpu.SemaphoreType.DMA((len(blocks),)),
        ],
        compiler_params=params(52),
        cost_estimate=cost(
            2 * ex_local * tall * width * (part + 2 * tok), 2 * ex_local * part * width
        ),
    )(place, routes_t, hidden, *blocks)


def kept(array):
    return pltpu.with_memory_space_constraint(array, pltpu.VMEM)


def outer_kernel(hidden, grads, out, total):
    chunk = pl.program_id(1)

    @pl.when(chunk == 0)
    def _():
        total[...] = jnp.zeros_like(total)

    total[...] += dot(hidden[0], grads[0], ((0,), (0,)))

    @pl.when(chunk == pl.num_programs(1) - 1)
    def _():
        out[0] = total[...].astype(bf16)


def outer(hidden, grads):
    ex_local, rows, part = hidden.shape
    width = grads.shape[2]
    tall = SUPER * MOST
    return pl.pallas_call(
        outer_kernel,
        grid=(ex_local, rows // tall),
        in_specs=[
            pl.BlockSpec((1, tall, part), lambda e, c: (e, c, 0)),
            pl.BlockSpec((1, tall, width), lambda e, c: (e, c, 0)),
        ],
        out_specs=pl.BlockSpec((1, part, width), lambda e, c: (e, 0, 0)),
        out_shape=jax.ShapeDtypeStruct((ex_local, part, width), bf16),
        scratch_shapes=[pltpu.VMEM((part, width), f32)],
        compiler_params=params(32),
    )(hidden, grads)


def finish_kernel(experts, routes_t, weights_t, returned, out):
    top_k, tok = routes_t.shape
    total = jnp.sum(returned[...], axis=0)
    total = jnp.concatenate([total, jnp.zeros((128 - MOST, 128), f32)], axis=0)
    total = total.T[:experts]
    _, slots = token_slots(routes_t[...], experts)
    slots = slots.astype(i32)
    found = jnp.zeros((experts, tok), f32)
    for m in range(MOST):
        found = jnp.where(slots == m, total[:, m : m + 1], found)
    numbers = iota((experts, tok), 0)
    for k in range(top_k):
        mine = jnp.where(routes_t[k : k + 1, :] == numbers, found, 0.0)
        mine = jnp.sum(mine, axis=0, keepdims=True)
        out[k : k + 1, :] = mine / weights_t[k : k + 1, :].astype(f32)


def finish(routes_t, weights_t, returned, experts):
    return pl.pallas_call(
        functools.partial(finish_kernel, experts),
        out_shape=jax.ShapeDtypeStruct(routes_t.shape, f32),
        compiler_params=params(24),
        cost_estimate=cost(10000, 100000),
    )(routes_t, weights_t, returned)


def hop(block, axis, flip):
    size = lax.axis_size(axis)
    return lax.ppermute(block, axis, [(i, i ^ flip) for i in range(size)])


def body(routes, combine, hidden, d_out, w_down):
    n_expert = lax.axis_size("expert")
    n_dp = lax.axis_size("dp")
    ex_local = w_down.shape[0]
    experts = n_expert * ex_local
    tok, top_k = routes.shape
    half = ex_local * MOST // 2
    routes_t, weights_t = routes.T, combine.T
    n_routes = tok * top_k
    me, mine = lax.axis_index("expert") * n_dp + lax.axis_index("dp"), lax.axis_index("expert")
    place = jnp.stack([me, mine * ex_local]).astype(i32)
    small = (n_expert, n_dp) == (4, 4)
    trade = lambda x: lax.all_to_all(x, GROUP, split_axis=0, concat_axis=0, tiled=True)
    if small:
        near = hop(d_out, "expert", 1)
        side = hop(d_out, "dp", 2)
        far = hop(d_out, "expert", 2)
        twin = hop(d_out, "dp", 1)
    else:
        twin = d_out
    sent, copies = pack(
        routes_t,
        routes.reshape(1, n_routes),
        combine.reshape(1, n_routes),
        hidden.reshape(n_routes, hidden.shape[2]),
        twin,
        n_expert,
        n_dp,
        half,
    )
    all_routes = trade(copies)
    if small:
        near_twin, side_twin, far_twin = [hop(x, "dp", 1) for x in (near, side, far)]
        early = [(0, d_out), (4, near), (2, side), (8, far)]
        early += [(1, twin), (5, near_twin), (3, side_twin), (9, far_twin)]
        near_side = hop(near, "dp", 2)
        far_side = hop(far, "dp", 2)
        both = hop(far, "expert", 1)
        received = trade(after(sent, near, side, far))
        orders = [[n for n, _ in early], [6, 10, 12, 14, 7, 11, 13, 15]]
        early = [x for _, x in early]
        backs = gather_back(place, orders, all_routes, w_down, early)
        both_side = hop(after(both, backs), "dp", 2)
        arranged = arrange(place, orders, received, ex_local)
        late = [near_side, far_side, both, after(both_side, arranged)]
        late += [hop(x, "dp", 1) for x in late]
        sums = gather_back(place, orders, all_routes, w_down, late, arranged, backs)
        d_w_down = gather_outer(place, orders, all_routes, arranged, early + late)
    else:
        received = trade(sent)
        grads = lax.all_gather(d_out, GROUP, axis=0, tiled=True)
        grads = gather(place, all_routes, grads, ex_local)
        arranged = arrange(place, [None], received, ex_local)
        sums = back(place, arranged, grads, w_down)
        d_w_down = outer(arranged, grads)
    d_combine = finish(routes_t, weights_t, trade(sums), experts)
    return d_w_down, d_combine.T


def solution(mesh):
    placed = (
        P(("groups", "expert", "dp"), None),
        P(("groups", "expert", "dp"), None),
        P(("groups", "expert", "dp"), None, None),
        P(("groups", "expert", "dp"), None),
        P("expert", "dp", None),
    )
    return jax.shard_map(
        body,
        mesh=mesh,
        in_specs=placed,
        out_specs=(P(("groups", "expert"), "dp", None), P(("groups", "expert", "dp"), None)),
        check_vma=False,
    )
```

```python
import functools

import jax
import jax.numpy as jnp
from jax import lax
from jax.experimental import pallas as pl
from jax.experimental.pallas import tpu as pltpu
import numpy as np
from jax.sharding import PartitionSpec as P

MOST = 18
SUPER = 8
TILES = 9
GROUP = ("expert", "dp")
f32, bf16, i32 = jnp.float32, jnp.bfloat16, jnp.int32


SMEM = pl.BlockSpec(memory_space=pltpu.SMEM)
VMEM = pl.BlockSpec(memory_space=pltpu.VMEM)
ANYWHERE = pl.BlockSpec(memory_space=pl.ANY)


def dot(a, b, dims=((1,), (0,))):
    return lax.dot_general(a, b, (dims, ((), ())), preferred_element_type=f32)


def iota(shape, dim):
    return lax.broadcasted_iota(i32, shape, dim)


def params(megabytes):
    return pltpu.CompilerParams(vmem_limit_bytes=megabytes * 2**20)


def cost(flops, nbytes):
    return pl.CostEstimate(flops=int(flops), bytes_accessed=int(nbytes), transcendentals=0)


def token_slots(routes_t, experts):
    top_k, tok = routes_t.shape
    numbers = iota((experts, tok), 0)
    named = jnp.zeros((experts, tok), f32)
    for k in range(top_k):
        named += jnp.where(routes_t[k : k + 1, :] == numbers, 1.0, 0.0)
    before = jnp.where(iota((tok, tok), 0) < iota((tok, tok), 1), 1.0, 0.0)
    return named, dot(named.astype(bf16), before.astype(bf16))


def pack_kernel(n_dp, half, routes_t, routes_flat, weights_flat, hidden, early, out, copies, target):
    del early
    ex = pl.program_id(0)
    experts = pl.num_programs(0) * 2 * half // MOST
    n_routes = routes_flat.shape[1]
    top_k, tok = routes_t.shape
    part = hidden.shape[1] // n_dp
    copies[...] = jnp.broadcast_to(routes_t[...][None], copies.shape)

    @pl.when(ex == 0)
    def _():
        _, slots = token_slots(routes_t[...], experts)
        shape = (tok, n_routes)
        spread = jnp.where(iota(shape, 1) // top_k == iota(shape, 0), 1.0, 0.0)
        slots = dot(slots.astype(bf16), spread.astype(bf16))
        numbers = iota((experts, n_routes), 0)
        rows = slots + (numbers * MOST).astype(f32)
        rows = jnp.where(routes_flat[...] == numbers, rows, 0.0)
        target[...] = jnp.sum(rows, axis=0, keepdims=True).astype(i32)

    weights = weights_flat[...].astype(f32)
    for side in range(2):
        first = ex * 2 * half + side * half
        chosen = target[...] - first == iota((half, n_routes), 0)
        chosen = jnp.where(chosen, weights, 0.0).astype(bf16)
        rows = dot(chosen, hidden[...]).astype(bf16)
        for d in range(n_dp):
            out[d, :, side * part : (side + 1) * part] = rows[:, d * part : (d + 1) * part]


def pack(routes_t, routes_flat, weights_flat, hidden, early, n_expert, n_dp, half):
    n_routes, units = hidden.shape
    part = units // n_dp
    whole = lambda shape: pl.BlockSpec(shape, lambda i: (0,) * len(shape))
    return pl.pallas_call(
        functools.partial(pack_kernel, n_dp, half),
        grid=(n_expert,),
        in_specs=[
            whole(routes_t.shape),
            whole(routes_flat.shape),
            whole(weights_flat.shape),
            whole(hidden.shape),
            pl.BlockSpec(memory_space=pl.ANY),
        ],
        out_specs=[
            pl.BlockSpec((n_dp, half, 2 * part), lambda i: (i, 0, 0)),
            pl.BlockSpec((n_dp,) + routes_t.shape, lambda i: (i, 0, 0)),
        ],
        out_shape=[
            jax.ShapeDtypeStruct((n_expert * n_dp, half, 2 * part), bf16),
            jax.ShapeDtypeStruct((n_expert * n_dp,) + routes_t.shape, i32),
        ],
        scratch_shapes=[pltpu.VMEM((1, n_routes), i32)],
        compiler_params=params(16),
        cost_estimate=cost(4 * n_expert * half * n_routes * units, 6 * n_routes * units),
    )(routes_t, routes_flat, weights_flat, hidden, early)


def after_kernel(*refs):
    pass


def after(array, *events):
    anywhere = pl.BlockSpec(memory_space=pl.ANY)
    return pl.pallas_call(
        after_kernel,
        in_specs=[anywhere] * (1 + len(events)),
        out_specs=anywhere,
        out_shape=jax.ShapeDtypeStruct(array.shape, array.dtype),
        input_output_aliases={0: 0},
    )(array, *events)


def tile_rows(i, rows):
    first = min(16 * i // MOST, SUPER - 2)
    place = 16 * i + iota((rows, 1), 0) % 16
    second = place >= MOST * (first + 1)
    slot = place - MOST * first - jnp.where(second, MOST, 0)
    return first, second, slot


def block_at(place, order, index):
    return place[0] ^ order[index] if order else pl.program_id(0) * SUPER + index


def gather_rows(order, place, routes_t, grads, out, start=0):
    tok = routes_t.shape[2]
    ex_local, _, width = out.shape
    rows = 16 * ex_local
    slots = []
    for b in range(SUPER):
        mine = routes_t[block_at(place, order, b)] - place[1]
        named, before = token_slots(mine, ex_local)
        slots.append(jnp.where(named > 0, before, -1.0))
    shape = (rows, ex_local)
    spread = jnp.where(iota(shape, 0) // 16 == iota(shape, 1), 1.0, 0.0).astype(bf16)
    step = min(512, width)
    for i in range(TILES):
        first, second, slot = tile_rows(i, rows)
        pair = jnp.concatenate([slots[first], slots[first + 1]], axis=1)
        pair = dot(spread, pair.astype(bf16))
        slot = slot.astype(f32)
        wanted = jnp.where(
            iota((rows, 2 * tok), 1) < tok,
            jnp.where(second, -5.0, slot),
            jnp.where(second, slot, -5.0),
        )
        chosen = jnp.where(pair == wanted, 1.0, 0.0).astype(bf16)
        near, far = grads(first), grads(first + 1)
        tile = start + 16 * i
        for c in range(0, width, step):
            here = slice(c, c + step)
            both = jnp.concatenate([near[:, here], far[:, here]], axis=0)
            found = dot(chosen, both).astype(bf16).reshape(ex_local, 16, step)
            out[:, tile : tile + 16, here] = found


def gather_kernel(place, routes_t, *refs):
    gather_rows(None, place, routes_t, lambda b: refs[b], refs[SUPER])


def gather(place, routes_t, grads, ex_local):
    blocks, top_k, tok = routes_t.shape
    width = grads.shape[1]
    tall = SUPER * MOST
    picked = lambda j: pl.BlockSpec((tok, width), lambda s: (SUPER * s + j, 0))
    return pl.pallas_call(
        gather_kernel,
        grid=(blocks // SUPER,),
        in_specs=[SMEM, pl.BlockSpec(routes_t.shape, lambda s: (0, 0, 0))]
        + [picked(j) for j in range(SUPER)],
        out_specs=pl.BlockSpec((ex_local, tall, width), lambda s: (0, s, 0)),
        out_shape=jax.ShapeDtypeStruct((ex_local, blocks * MOST, width), bf16),
        compiler_params=params(48),
    )(place, routes_t, *([grads] * SUPER))


def fetch(sources, held, sems):
    copies = [
        pltpu.make_async_copy(source, held.at[i], sems.at[i]) for i, source in enumerate(sources)
    ]
    for copy in copies:
        copy.start()
    waited = set()

    def block(i):
        if i not in waited:
            copies[i].wait()
            waited.add(i)
        return held.at[i]

    return block


def arrange_kernel(orders, ex_local, place, received, out):
    _, half, double = received.shape
    part = double // 2
    paired = ex_local % 2 == 0
    some = ex_local // 2 if paired else ex_local
    rows = 16 * some
    expert = iota((rows, 1), 0) // 16
    for i in range(TILES):
        first, second, slot = tile_rows(i, rows)
        block = jnp.where(second, half, 0)
        chosen = []
        for side in range(1 if paired else 2):
            spot = expert * MOST + slot - side * half
            column = jnp.where((spot >= 0) & (spot < half), block + spot, -1)
            hit = iota((rows, 2 * half), 1) == column
            chosen.append(jnp.where(hit, 1.0, 0.0).astype(bf16))
        for piece, order in enumerate(orders):
            pair = [received[block_at(place, order, first + b)] for b in range(2)]
            pair = jnp.concatenate(pair, axis=0)
            results = [dot(c, pair) for c in chosen]
            if paired:
                sides = [results[0][:, :part], results[0][:, part:]]
            else:
                sides = [results[0][:, :part] + results[1][:, part:]]
            tile = piece * SUPER * MOST + 16 * i
            for s, found in enumerate(sides):
                here = slice(s * some, (s + 1) * some)
                out[here, tile : tile + 16, :] = found.astype(bf16).reshape(some, 16, part)


def arrange(place, orders, received, ex_local):
    blocks, half, double = received.shape
    part = double // 2
    shape = (ex_local, blocks * MOST, part)
    kernel = functools.partial(arrange_kernel, orders, ex_local)
    if orders[0]:
        return pl.pallas_call(
            kernel,
            in_specs=[SMEM, VMEM],
            out_specs=VMEM,
            out_shape=jax.ShapeDtypeStruct(shape, bf16),
            compiler_params=params(24),
            cost_estimate=cost(4 * ex_local * blocks * MOST * half * double, 2**22),
        )(place, received)
    return pl.pallas_call(
        kernel,
        grid=(blocks // SUPER,),
        in_specs=[SMEM, pl.BlockSpec(received.shape, lambda s: (0, 0, 0))],
        out_specs=pl.BlockSpec((ex_local, SUPER * MOST, part), lambda s: (0, s, 0)),
        out_shape=jax.ShapeDtypeStruct(shape, bf16),
        compiler_params=params(32),
    )(place, received)


def back_rows(place, expert, hidden, grads, weights, sums):
    found = dot(grads, weights, ((1,), (1,)))
    total = jnp.sum(hidden.astype(f32) * found, axis=1, keepdims=True)
    sums[...] += jnp.where(iota(sums.shape, 1) == place[1] + expert, total, 0.0)


def back_kernel(place, hidden, grads, weights, out, sums):
    expert = pl.program_id(1)

    @pl.when(expert == 0)
    def _():
        sums[...] = jnp.zeros_like(sums)

    back_rows(place, expert, hidden[0], grads[0], weights[0], sums)

    @pl.when(expert == pl.num_programs(1) - 1)
    def _():
        for b in range(SUPER):
            out[b] = sums[b * MOST : (b + 1) * MOST, :]


def back(place, hidden, grads, weights):
    ex_local, rows, width = grads.shape
    part = weights.shape[1]
    tall = SUPER * MOST
    return pl.pallas_call(
        back_kernel,
        grid=(rows // tall, ex_local),
        in_specs=[
            SMEM,
            pl.BlockSpec((1, tall, part), lambda s, e: (e, s, 0)),
            pl.BlockSpec((1, tall, width), lambda s, e: (e, s, 0)),
            pl.BlockSpec((1, part, width), lambda s, e: (e, 0, 0)),
        ],
        out_specs=pl.BlockSpec((SUPER, MOST, 128), lambda s, e: (s, 0, 0)),
        out_shape=jax.ShapeDtypeStruct((rows // MOST, MOST, 128), f32),
        scratch_shapes=[pltpu.VMEM((tall, 128), f32)],
        compiler_params=params(32),
    )(place, hidden, grads, weights)


def early_kernel(order, place, routes_t, weights, *refs):
    blocks, (out, held, rows, sems) = refs[:SUPER], refs[SUPER:]
    step = pl.program_id(0)

    @pl.when(step == 0)
    def _():
        gather_rows(order, place, routes_t, fetch(blocks, held, sems), rows)

    for j in range(GROUPED):
        out[j] = dot(rows[step * GROUPED + j], weights[j], ((1,), (1,)))


def early_products(place, order, routes_t, weights, blocks):
    ex_local, part, width = weights.shape
    tok = blocks[0].shape[0]
    tall = SUPER * MOST
    grouped = lambda rows, columns: pl.BlockSpec((GROUPED, rows, columns), lambda e: (e, 0, 0))
    return pl.pallas_call(
        functools.partial(early_kernel, order),
        grid=(ex_local // GROUPED,),
        in_specs=[SMEM, VMEM, grouped(part, width)] + [ANYWHERE] * SUPER,
        out_specs=grouped(tall, part),
        out_shape=jax.ShapeDtypeStruct((ex_local, tall, part), f32),
        scratch_shapes=[
            pltpu.VMEM((SUPER, tok, width), bf16),
            pltpu.VMEM((ex_local, tall, width), bf16),
            pltpu.SemaphoreType.DMA((SUPER,)),
        ],
        compiler_params=params(40),
        cost_estimate=cost(
            2 * ex_local * tall * width * (part + 2 * tok), 2 * ex_local * part * width
        ),
    )(place, routes_t, weights, *blocks)


GROUPED = 2


def gradients_kernel(orders, place, routes_t, weights, hidden, backs, *refs):
    count = SUPER * len(orders)
    blocks, (out, summed, sums, held, rows, sems) = refs[:count], refs[count:]
    step = pl.program_id(0)
    tall = SUPER * MOST
    width = out.shape[2]
    columns = min(512, width)

    @pl.when(step == 0)
    def _():
        sums[...] = jnp.zeros_like(sums)
        block = fetch(blocks, held, sems)
        for piece, order in enumerate(orders):
            mine = lambda b, piece=piece: block(piece * SUPER + b)
            gather_rows(order, place, routes_t, mine, rows, piece * tall)

    lane = iota((tall, 128), 1) - place[1]
    for j in range(GROUPED):
        expert = step * GROUPED + j
        found = hidden[j, :tall, :].astype(f32) * backs[j]
        total = jnp.sum(found, axis=1, keepdims=True)
        sums[:tall, :] += jnp.where(lane == expert, total, 0.0)
        late = hidden[j, tall:, :]
        found = jnp.zeros((tall, 128), f32)
        for c in range(0, width, columns):
            here = slice(c, c + columns)
            product = dot(hidden[j], rows[expert, :, here], ((0,), (0,)))
            out[j, :, here] = product.astype(bf16)
            part = dot(late, weights[j, :, here]) * rows[expert, tall:, here].astype(f32)
            for piece in range(0, columns, 128):
                found += part[:, piece : piece + 128]
        total = jnp.sum(found, axis=1, keepdims=True)
        sums[tall:, :] += jnp.where(lane == expert, total, 0.0)

    @pl.when(step == pl.num_programs(0) - 1)
    def _():
        for i, order in enumerate(orders):
            for b in range(SUPER):
                start = (i * SUPER + b) * MOST
                summed[block_at(place, order, b)] = sums[start : start + MOST, :]


def gradients(place, orders, routes_t, weights, hidden, backs, blocks):
    ex_local, part, width = weights.shape
    rows = hidden.shape[1]
    tok = blocks[0].shape[0]
    count = len(blocks)
    grouped = lambda rows, columns: pl.BlockSpec((GROUPED, rows, columns), lambda e: (e, 0, 0))
    return pl.pallas_call(
        functools.partial(gradients_kernel, orders),
        grid=(ex_local // GROUPED,),
        in_specs=[
            SMEM,
            VMEM,
            grouped(part, width),
            grouped(rows, part),
            grouped(SUPER * MOST, part),
        ]
        + [ANYWHERE] * count,
        out_specs=[
            grouped(part, width),
            pl.BlockSpec((count, MOST, 128), lambda e: (0, 0, 0)),
        ],
        out_shape=[
            jax.ShapeDtypeStruct((ex_local, part, width), bf16),
            jax.ShapeDtypeStruct((count, MOST, 128), f32),
        ],
        scratch_shapes=[
            pltpu.VMEM((rows, 128), f32),
            pltpu.VMEM((count, tok, width), bf16),
            pltpu.VMEM((ex_local, rows, width), bf16),
            pltpu.SemaphoreType.DMA((count,)),
        ],
        compiler_params=params(56),
        cost_estimate=cost(
            2 * ex_local * rows * width * (2 * part + 2 * tok), 4 * ex_local * part * width
        ),
    )(place, routes_t, weights, hidden, backs, *blocks)


def outer_kernel(hidden, grads, out, total):
    chunk = pl.program_id(1)

    @pl.when(chunk == 0)
    def _():
        total[...] = jnp.zeros_like(total)

    total[...] += dot(hidden[0], grads[0], ((0,), (0,)))

    @pl.when(chunk == pl.num_programs(1) - 1)
    def _():
        out[0] = total[...].astype(bf16)


def outer(hidden, grads):
    ex_local, rows, part = hidden.shape
    width = grads.shape[2]
    tall = SUPER * MOST
    return pl.pallas_call(
        outer_kernel,
        grid=(ex_local, rows // tall),
        in_specs=[
            pl.BlockSpec((1, tall, part), lambda e, c: (e, c, 0)),
            pl.BlockSpec((1, tall, width), lambda e, c: (e, c, 0)),
        ],
        out_specs=pl.BlockSpec((1, part, width), lambda e, c: (e, 0, 0)),
        out_shape=jax.ShapeDtypeStruct((ex_local, part, width), bf16),
        scratch_shapes=[pltpu.VMEM((part, width), f32)],
        compiler_params=params(32),
    )(hidden, grads)


def finish_kernel(experts, routes_t, weights_t, returned, out):
    top_k, tok = routes_t.shape
    total = jnp.sum(returned[...], axis=0)
    total = jnp.concatenate([total, jnp.zeros((128 - MOST, 128), f32)], axis=0)
    total = total.T[:experts]
    _, slots = token_slots(routes_t[...], experts)
    slots = slots.astype(i32)
    found = jnp.zeros((experts, tok), f32)
    for m in range(MOST):
        found = jnp.where(slots == m, total[:, m : m + 1], found)
    numbers = iota((experts, tok), 0)
    for k in range(top_k):
        mine = jnp.where(routes_t[k : k + 1, :] == numbers, found, 0.0)
        mine = jnp.sum(mine, axis=0, keepdims=True)
        out[k : k + 1, :] = mine / weights_t[k : k + 1, :].astype(f32)


def finish(routes_t, weights_t, returned, experts):
    return pl.pallas_call(
        functools.partial(finish_kernel, experts),
        out_shape=jax.ShapeDtypeStruct(routes_t.shape, f32),
        compiler_params=params(24),
        cost_estimate=cost(10000, 100000),
    )(routes_t, weights_t, returned)


def hop(block, axis, flip):
    size = lax.axis_size(axis)
    return lax.ppermute(block, axis, [(i, i ^ flip) for i in range(size)])


def body(routes, combine, hidden, d_out, w_down):
    n_expert = lax.axis_size("expert")
    n_dp = lax.axis_size("dp")
    ex_local = w_down.shape[0]
    experts = n_expert * ex_local
    tok, top_k = routes.shape
    half = ex_local * MOST // 2
    routes_t, weights_t = routes.T, combine.T
    n_routes = tok * top_k
    me, mine = lax.axis_index("expert") * n_dp + lax.axis_index("dp"), lax.axis_index("expert")
    place = jnp.stack([me, mine * ex_local]).astype(i32)
    small = (n_expert, n_dp) == (4, 4)
    trade = lambda x: lax.all_to_all(x, GROUP, split_axis=0, concat_axis=0, tiled=True)
    if small:
        near = hop(d_out, "expert", 1)
        side = hop(d_out, "dp", 2)
        far = hop(d_out, "expert", 2)
        twin = hop(d_out, "dp", 1)
    else:
        twin = d_out
    sent, copies = pack(
        routes_t,
        routes.reshape(1, n_routes),
        combine.reshape(1, n_routes),
        hidden.reshape(n_routes, hidden.shape[2]),
        twin,
        n_expert,
        n_dp,
        half,
    )
    all_routes = trade(copies)
    if small:
        near_twin, side_twin, far_twin = [hop(x, "dp", 1) for x in (near, side, far)]
        early = [(0, d_out), (4, near), (2, side), (8, far)]
        early += [(1, twin), (5, near_twin), (3, side_twin), (9, far_twin)]
        near_side = hop(near, "dp", 2)
        far_side = hop(far, "dp", 2)
        both = hop(far, "expert", 1)
        received = trade(after(sent, near, side, far))
        orders = [[n for n, _ in early], [6, 10, 12, 14, 7, 11, 13, 15]]
        early = [x for _, x in early]
        backs = early_products(place, orders[0], all_routes, w_down, early)
        both = after(both, backs)
        both_side = hop(both, "dp", 2)
        arranged = arrange(place, orders, received, ex_local)
        late = [near_side, far_side, both, after(both_side, arranged)]
        late += [hop(x, "dp", 1) for x in late]
        d_w_down, sums = gradients(
            place, orders, all_routes, w_down, arranged, backs, early + late
        )
    else:
        received = trade(sent)
        grads = lax.all_gather(d_out, GROUP, axis=0, tiled=True)
        grads = gather(place, all_routes, grads, ex_local)
        arranged = arrange(place, [None], received, ex_local)
        sums = back(place, arranged, grads, w_down)
        d_w_down = outer(arranged, grads)
    d_combine = finish(routes_t, weights_t, trade(sums), experts)
    return d_w_down, d_combine.T


def solution(mesh):
    placed = (
        P(("groups", "expert", "dp"), None),
        P(("groups", "expert", "dp"), None),
        P(("groups", "expert", "dp"), None, None),
        P(("groups", "expert", "dp"), None),
        P("expert", "dp", None),
    )
    return jax.shard_map(
        body,
        mesh=mesh,
        in_specs=placed,
        out_specs=(P(("groups", "expert"), "dp", None), P(("groups", "expert", "dp"), None)),
        check_vma=False,
    )
```

```python
import functools

import jax
import jax.numpy as jnp
from jax import lax
from jax.experimental import pallas as pl
from jax.experimental.pallas import tpu as pltpu
import numpy as np
from jax.sharding import PartitionSpec as P

MOST = 18
SUPER = 8
TILES = 9
GROUP = ("expert", "dp")
f32, bf16, i32 = jnp.float32, jnp.bfloat16, jnp.int32


SMEM = pl.BlockSpec(memory_space=pltpu.SMEM)
VMEM = pl.BlockSpec(memory_space=pltpu.VMEM)
ANYWHERE = pl.BlockSpec(memory_space=pl.ANY)


def dot(a, b, dims=((1,), (0,))):
    return lax.dot_general(a, b, (dims, ((), ())), preferred_element_type=f32)


def iota(shape, dim):
    return lax.broadcasted_iota(i32, shape, dim)


def params(megabytes):
    return pltpu.CompilerParams(vmem_limit_bytes=megabytes * 2**20)


def cost(flops, nbytes):
    return pl.CostEstimate(flops=int(flops), bytes_accessed=int(nbytes), transcendentals=0)


def token_slots(routes_t, experts):
    top_k, tok = routes_t.shape
    numbers = iota((experts, tok), 0)
    named = jnp.zeros((experts, tok), f32)
    for k in range(top_k):
        named += jnp.where(routes_t[k : k + 1, :] == numbers, 1.0, 0.0)
    before = jnp.where(iota((tok, tok), 0) < iota((tok, tok), 1), 1.0, 0.0)
    return named, dot(named.astype(bf16), before.astype(bf16))


def pack_kernel(n_dp, half, routes_t, routes_flat, weights_flat, hidden, early, out, copies, target):
    del early
    ex = pl.program_id(0)
    experts = pl.num_programs(0) * 2 * half // MOST
    n_routes = routes_flat.shape[1]
    top_k, tok = routes_t.shape
    part = hidden.shape[1] // n_dp
    copies[...] = jnp.broadcast_to(routes_t[...][None], copies.shape)

    @pl.when(ex == 0)
    def _():
        _, slots = token_slots(routes_t[...], experts)
        shape = (tok, n_routes)
        spread = jnp.where(iota(shape, 1) // top_k == iota(shape, 0), 1.0, 0.0)
        slots = dot(slots.astype(bf16), spread.astype(bf16))
        numbers = iota((experts, n_routes), 0)
        rows = slots + (numbers * MOST).astype(f32)
        rows = jnp.where(routes_flat[...] == numbers, rows, 0.0)
        target[...] = jnp.sum(rows, axis=0, keepdims=True).astype(i32)

    weights = weights_flat[...].astype(f32)
    for side in range(2):
        first = ex * 2 * half + side * half
        chosen = target[...] - first == iota((half, n_routes), 0)
        chosen = jnp.where(chosen, weights, 0.0).astype(bf16)
        rows = dot(chosen, hidden[...]).astype(bf16)
        for d in range(n_dp):
            out[d, :, side * part : (side + 1) * part] = rows[:, d * part : (d + 1) * part]


def pack(routes_t, routes_flat, weights_flat, hidden, early, n_expert, n_dp, half):
    n_routes, units = hidden.shape
    part = units // n_dp
    whole = lambda shape: pl.BlockSpec(shape, lambda i: (0,) * len(shape))
    return pl.pallas_call(
        functools.partial(pack_kernel, n_dp, half),
        grid=(n_expert,),
        in_specs=[
            whole(routes_t.shape),
            whole(routes_flat.shape),
            whole(weights_flat.shape),
            whole(hidden.shape),
            pl.BlockSpec(memory_space=pl.ANY),
        ],
        out_specs=[
            pl.BlockSpec((n_dp, half, 2 * part), lambda i: (i, 0, 0)),
            pl.BlockSpec((n_dp,) + routes_t.shape, lambda i: (i, 0, 0)),
        ],
        out_shape=[
            jax.ShapeDtypeStruct((n_expert * n_dp, half, 2 * part), bf16),
            jax.ShapeDtypeStruct((n_expert * n_dp,) + routes_t.shape, i32),
        ],
        scratch_shapes=[pltpu.VMEM((1, n_routes), i32)],
        compiler_params=params(16),
        cost_estimate=cost(4 * n_expert * half * n_routes * units, 6 * n_routes * units),
    )(routes_t, routes_flat, weights_flat, hidden, early)


def after_kernel(*refs):
    pass


def after(array, *events):
    anywhere = pl.BlockSpec(memory_space=pl.ANY)
    return pl.pallas_call(
        after_kernel,
        in_specs=[anywhere] * (1 + len(events)),
        out_specs=anywhere,
        out_shape=jax.ShapeDtypeStruct(array.shape, array.dtype),
        input_output_aliases={0: 0},
    )(array, *events)


def tile_rows(i, rows):
    first = min(16 * i // MOST, SUPER - 2)
    place = 16 * i + iota((rows, 1), 0) % 16
    second = place >= MOST * (first + 1)
    slot = place - MOST * first - jnp.where(second, MOST, 0)
    return first, second, slot


def block_at(place, order, index):
    return place[0] ^ order[index] if order else pl.program_id(0) * SUPER + index


def gather_rows(order, place, routes_t, grads, out, start=0):
    tok = routes_t.shape[2]
    ex_local, _, width = out.shape
    rows = 16 * ex_local
    slots = []
    for b in range(SUPER):
        mine = routes_t[block_at(place, order, b)] - place[1]
        named, before = token_slots(mine, ex_local)
        slots.append(jnp.where(named > 0, before, -1.0))
    shape = (rows, ex_local)
    spread = jnp.where(iota(shape, 0) // 16 == iota(shape, 1), 1.0, 0.0).astype(bf16)
    step = min(512, width)
    for i in range(TILES):
        first, second, slot = tile_rows(i, rows)
        pair = jnp.concatenate([slots[first], slots[first + 1]], axis=1)
        pair = dot(spread, pair.astype(bf16))
        slot = slot.astype(f32)
        wanted = jnp.where(
            iota((rows, 2 * tok), 1) < tok,
            jnp.where(second, -5.0, slot),
            jnp.where(second, slot, -5.0),
        )
        chosen = jnp.where(pair == wanted, 1.0, 0.0).astype(bf16)
        near, far = grads(first), grads(first + 1)
        tile = start + 16 * i
        for c in range(0, width, step):
            here = slice(c, c + step)
            both = jnp.concatenate([near[:, here], far[:, here]], axis=0)
            found = dot(chosen, both).astype(bf16).reshape(ex_local, 16, step)
            out[:, tile : tile + 16, here] = found


def gather_kernel(place, routes_t, *refs):
    gather_rows(None, place, routes_t, lambda b: refs[b], refs[SUPER])


def gather(place, routes_t, grads, ex_local):
    blocks, top_k, tok = routes_t.shape
    width = grads.shape[1]
    tall = SUPER * MOST
    picked = lambda j: pl.BlockSpec((tok, width), lambda s: (SUPER * s + j, 0))
    return pl.pallas_call(
        gather_kernel,
        grid=(blocks // SUPER,),
        in_specs=[SMEM, pl.BlockSpec(routes_t.shape, lambda s: (0, 0, 0))]
        + [picked(j) for j in range(SUPER)],
        out_specs=pl.BlockSpec((ex_local, tall, width), lambda s: (0, s, 0)),
        out_shape=jax.ShapeDtypeStruct((ex_local, blocks * MOST, width), bf16),
        compiler_params=params(48),
    )(place, routes_t, *([grads] * SUPER))


def fetch(sources, held, sems):
    copies = [
        pltpu.make_async_copy(source, held.at[i], sems.at[i]) for i, source in enumerate(sources)
    ]
    for copy in copies:
        copy.start()
    waited = set()

    def block(i):
        if i not in waited:
            copies[i].wait()
            waited.add(i)
        return held.at[i]

    return block


def arrange_kernel(orders, ex_local, place, received, out):
    _, half, double = received.shape
    part = double // 2
    paired = ex_local % 2 == 0
    some = ex_local // 2 if paired else ex_local
    rows = 16 * some
    expert = iota((rows, 1), 0) // 16
    for i in range(TILES):
        first, second, slot = tile_rows(i, rows)
        block = jnp.where(second, half, 0)
        chosen = []
        for side in range(1 if paired else 2):
            spot = expert * MOST + slot - side * half
            column = jnp.where((spot >= 0) & (spot < half), block + spot, -1)
            hit = iota((rows, 2 * half), 1) == column
            chosen.append(jnp.where(hit, 1.0, 0.0).astype(bf16))
        for piece, order in enumerate(orders):
            pair = [received[block_at(place, order, first + b)] for b in range(2)]
            pair = jnp.concatenate(pair, axis=0)
            results = [dot(c, pair) for c in chosen]
            if paired:
                sides = [results[0][:, :part], results[0][:, part:]]
            else:
                sides = [results[0][:, :part] + results[1][:, part:]]
            tile = piece * SUPER * MOST + 16 * i
            for s, found in enumerate(sides):
                here = slice(s * some, (s + 1) * some)
                out[here, tile : tile + 16, :] = found.astype(bf16).reshape(some, 16, part)


def arrange(place, orders, received, ex_local):
    blocks, half, double = received.shape
    part = double // 2
    shape = (ex_local, blocks * MOST, part)
    kernel = functools.partial(arrange_kernel, orders, ex_local)
    if orders[0]:
        return pl.pallas_call(
            kernel,
            in_specs=[SMEM, VMEM],
            out_specs=VMEM,
            out_shape=jax.ShapeDtypeStruct(shape, bf16),
            compiler_params=params(24),
            cost_estimate=cost(4 * ex_local * blocks * MOST * half * double, 2**22),
        )(place, received)
    return pl.pallas_call(
        kernel,
        grid=(blocks // SUPER,),
        in_specs=[SMEM, pl.BlockSpec(received.shape, lambda s: (0, 0, 0))],
        out_specs=pl.BlockSpec((ex_local, SUPER * MOST, part), lambda s: (0, s, 0)),
        out_shape=jax.ShapeDtypeStruct(shape, bf16),
        compiler_params=params(32),
    )(place, received)


def back_rows(place, expert, hidden, grads, weights, sums):
    found = dot(grads, weights, ((1,), (1,)))
    total = jnp.sum(hidden.astype(f32) * found, axis=1, keepdims=True)
    sums[...] += jnp.where(iota(sums.shape, 1) == place[1] + expert, total, 0.0)


def back_kernel(place, hidden, grads, weights, out, sums):
    expert = pl.program_id(1)

    @pl.when(expert == 0)
    def _():
        sums[...] = jnp.zeros_like(sums)

    back_rows(place, expert, hidden[0], grads[0], weights[0], sums)

    @pl.when(expert == pl.num_programs(1) - 1)
    def _():
        for b in range(SUPER):
            out[b] = sums[b * MOST : (b + 1) * MOST, :]


def back(place, hidden, grads, weights):
    ex_local, rows, width = grads.shape
    part = weights.shape[1]
    tall = SUPER * MOST
    return pl.pallas_call(
        back_kernel,
        grid=(rows // tall, ex_local),
        in_specs=[
            SMEM,
            pl.BlockSpec((1, tall, part), lambda s, e: (e, s, 0)),
            pl.BlockSpec((1, tall, width), lambda s, e: (e, s, 0)),
            pl.BlockSpec((1, part, width), lambda s, e: (e, 0, 0)),
        ],
        out_specs=pl.BlockSpec((SUPER, MOST, 128), lambda s, e: (s, 0, 0)),
        out_shape=jax.ShapeDtypeStruct((rows // MOST, MOST, 128), f32),
        scratch_shapes=[pltpu.VMEM((tall, 128), f32)],
        compiler_params=params(32),
    )(place, hidden, grads, weights)


def early_kernel(order, place, routes_t, weights, *refs):
    blocks, (out, kept_rows, held, rows, sems) = refs[:SUPER], refs[SUPER:]
    step = pl.program_id(0)

    @pl.when(step == 0)
    def _():
        gather_rows(order, place, routes_t, fetch(blocks, held, sems), rows)

    for j in range(GROUPED):
        mine = rows[step * GROUPED + j]
        kept_rows[j] = mine
        out[j] = dot(mine, weights[j], ((1,), (1,)))


def early_products(place, order, routes_t, weights, blocks):
    ex_local, part, width = weights.shape
    tok = blocks[0].shape[0]
    tall = SUPER * MOST
    grouped = lambda rows, columns: pl.BlockSpec((GROUPED, rows, columns), lambda e: (e, 0, 0))
    return pl.pallas_call(
        functools.partial(early_kernel, order),
        grid=(ex_local // GROUPED,),
        in_specs=[SMEM, VMEM, grouped(part, width)] + [ANYWHERE] * SUPER,
        out_specs=[grouped(tall, part), grouped(tall, width)],
        out_shape=[
            jax.ShapeDtypeStruct((ex_local, tall, part), f32),
            jax.ShapeDtypeStruct((ex_local, tall, width), bf16),
        ],
        scratch_shapes=[
            pltpu.VMEM((SUPER, tok, width), bf16),
            pltpu.VMEM((ex_local, tall, width), bf16),
            pltpu.SemaphoreType.DMA((SUPER,)),
        ],
        compiler_params=params(40),
        cost_estimate=cost(
            2 * ex_local * tall * width * (part + 2 * tok), 2 * ex_local * part * width
        ),
    )(place, routes_t, weights, *blocks)


GROUPED = 4


def gradients_kernel(orders, place, routes_t, weights, hidden, backs, early, *refs):
    count = SUPER
    blocks, (out, summed, sums, held, rows, sems) = refs[:count], refs[count:]
    step = pl.program_id(0)
    tall = SUPER * MOST
    width = out.shape[2]
    columns = min(512, width)

    @pl.when(step == 0)
    def _():
        sums[...] = jnp.zeros_like(sums)
        gather_rows(orders[1], place, routes_t, fetch(blocks, held, sems), rows)

    lane = iota((tall, 128), 1) - place[1]
    for j in range(GROUPED):
        expert = step * GROUPED + j
        found = hidden[j, :tall, :].astype(f32) * backs[j]
        total = jnp.sum(found, axis=1, keepdims=True)
        sums[:tall, :] += jnp.where(lane == expert, total, 0.0)
        late = hidden[j, tall:, :]
        found = jnp.zeros((tall, 128), f32)
        for c in range(0, width, columns):
            here = slice(c, c + columns)
            mine = rows[expert, :, here]
            both = jnp.concatenate([early[j, :, here], mine], axis=0)
            product = dot(hidden[j], both, ((0,), (0,)))
            out[j, :, here] = product.astype(bf16)
            part = dot(late, weights[j, :, here]) * mine.astype(f32)
            for piece in range(0, columns, 128):
                found += part[:, piece : piece + 128]
        total = jnp.sum(found, axis=1, keepdims=True)
        sums[tall:, :] += jnp.where(lane == expert, total, 0.0)

    @pl.when(step == pl.num_programs(0) - 1)
    def _():
        for i, order in enumerate(orders):
            for b in range(SUPER):
                start = (i * SUPER + b) * MOST
                summed[block_at(place, order, b)] = sums[start : start + MOST, :]


def gradients(place, orders, routes_t, weights, hidden, backs, early, blocks):
    ex_local, part, width = weights.shape
    rows = hidden.shape[1]
    tok = blocks[0].shape[0]
    tall = SUPER * MOST
    count = 2 * SUPER
    grouped = lambda rows, columns: pl.BlockSpec((GROUPED, rows, columns), lambda e: (e, 0, 0))
    return pl.pallas_call(
        functools.partial(gradients_kernel, orders),
        grid=(ex_local // GROUPED,),
        in_specs=[
            SMEM,
            VMEM,
            grouped(part, width),
            grouped(rows, part),
            grouped(tall, part),
            grouped(tall, width),
        ]
        + [ANYWHERE] * SUPER,
        out_specs=[
            grouped(part, width),
            pl.BlockSpec((count, MOST, 128), lambda e: (0, 0, 0)),
        ],
        out_shape=[
            jax.ShapeDtypeStruct((ex_local, part, width), bf16),
            jax.ShapeDtypeStruct((count, MOST, 128), f32),
        ],
        scratch_shapes=[
            pltpu.VMEM((rows, 128), f32),
            pltpu.VMEM((SUPER, tok, width), bf16),
            pltpu.VMEM((ex_local, tall, width), bf16),
            pltpu.SemaphoreType.DMA((SUPER,)),
        ],
        compiler_params=params(56),
        cost_estimate=cost(
            2 * ex_local * rows * width * (2 * part + 2 * tok), 4 * ex_local * part * width
        ),
    )(place, routes_t, weights, hidden, backs, early, *blocks)


def outer_kernel(hidden, grads, out, total):
    chunk = pl.program_id(1)

    @pl.when(chunk == 0)
    def _():
        total[...] = jnp.zeros_like(total)

    total[...] += dot(hidden[0], grads[0], ((0,), (0,)))

    @pl.when(chunk == pl.num_programs(1) - 1)
    def _():
        out[0] = total[...].astype(bf16)


def outer(hidden, grads):
    ex_local, rows, part = hidden.shape
    width = grads.shape[2]
    tall = SUPER * MOST
    return pl.pallas_call(
        outer_kernel,
        grid=(ex_local, rows // tall),
        in_specs=[
            pl.BlockSpec((1, tall, part), lambda e, c: (e, c, 0)),
            pl.BlockSpec((1, tall, width), lambda e, c: (e, c, 0)),
        ],
        out_specs=pl.BlockSpec((1, part, width), lambda e, c: (e, 0, 0)),
        out_shape=jax.ShapeDtypeStruct((ex_local, part, width), bf16),
        scratch_shapes=[pltpu.VMEM((part, width), f32)],
        compiler_params=params(32),
    )(hidden, grads)


def finish_kernel(experts, routes_t, weights_t, returned, out):
    top_k, tok = routes_t.shape
    total = jnp.sum(returned[...], axis=0)
    total = jnp.concatenate([total, jnp.zeros((128 - MOST, 128), f32)], axis=0)
    total = total.T[:experts]
    _, slots = token_slots(routes_t[...], experts)
    slots = slots.astype(i32)
    found = jnp.zeros((experts, tok), f32)
    for m in range(MOST):
        found = jnp.where(slots == m, total[:, m : m + 1], found)
    numbers = iota((experts, tok), 0)
    for k in range(top_k):
        mine = jnp.where(routes_t[k : k + 1, :] == numbers, found, 0.0)
        mine = jnp.sum(mine, axis=0, keepdims=True)
        out[k : k + 1, :] = mine / weights_t[k : k + 1, :].astype(f32)


def finish(routes_t, weights_t, returned, experts):
    return pl.pallas_call(
        functools.partial(finish_kernel, experts),
        out_shape=jax.ShapeDtypeStruct(routes_t.shape, f32),
        compiler_params=params(24),
        cost_estimate=cost(10000, 100000),
    )(routes_t, weights_t, returned)


def hop(block, axis, flip):
    size = lax.axis_size(axis)
    return lax.ppermute(block, axis, [(i, i ^ flip) for i in range(size)])


def body(routes, combine, hidden, d_out, w_down):
    n_expert = lax.axis_size("expert")
    n_dp = lax.axis_size("dp")
    ex_local = w_down.shape[0]
    experts = n_expert * ex_local
    tok, top_k = routes.shape
    half = ex_local * MOST // 2
    routes_t, weights_t = routes.T, combine.T
    n_routes = tok * top_k
    me, mine = lax.axis_index("expert") * n_dp + lax.axis_index("dp"), lax.axis_index("expert")
    place = jnp.stack([me, mine * ex_local]).astype(i32)
    small = (n_expert, n_dp) == (4, 4)
    trade = lambda x: lax.all_to_all(x, GROUP, split_axis=0, concat_axis=0, tiled=True)
    if small:
        near = hop(d_out, "expert", 1)
        side = hop(d_out, "dp", 2)
        far = hop(d_out, "expert", 2)
        twin = hop(d_out, "dp", 1)
    else:
        twin = d_out
    sent, copies = pack(
        routes_t,
        routes.reshape(1, n_routes),
        combine.reshape(1, n_routes),
        hidden.reshape(n_routes, hidden.shape[2]),
        twin,
        n_expert,
        n_dp,
        half,
    )
    all_routes = trade(copies)
    if small:
        near_twin, side_twin, far_twin = [hop(x, "dp", 1) for x in (near, side, far)]
        early = [(0, d_out), (4, near), (2, side), (8, far)]
        early += [(1, twin), (5, near_twin), (3, side_twin), (9, far_twin)]
        near_side = hop(near, "dp", 2)
        far_side = hop(far, "dp", 2)
        both = hop(far, "expert", 1)
        received = trade(after(sent, near, side, far))
        orders = [[n for n, _ in early], [6, 10, 12, 14, 7, 11, 13, 15]]
        early = [x for _, x in early]
        backs, rows = early_products(place, orders[0], all_routes, w_down, early)
        both = after(both, backs)
        both_side = hop(both, "dp", 2)
        arranged = arrange(place, orders, received, ex_local)
        late = [near_side, far_side, both, after(both_side, arranged)]
        late += [hop(x, "dp", 1) for x in late]
        d_w_down, sums = gradients(
            place, orders, all_routes, w_down, arranged, backs, rows, late
        )
    else:
        received = trade(sent)
        grads = lax.all_gather(d_out, GROUP, axis=0, tiled=True)
        grads = gather(place, all_routes, grads, ex_local)
        arranged = arrange(place, [None], received, ex_local)
        sums = back(place, arranged, grads, w_down)
        d_w_down = outer(arranged, grads)
    d_combine = finish(routes_t, weights_t, trade(sums), experts)
    return d_w_down, d_combine.T


def solution(mesh):
    placed = (
        P(("groups", "expert", "dp"), None),
        P(("groups", "expert", "dp"), None),
        P(("groups", "expert", "dp"), None, None),
        P(("groups", "expert", "dp"), None),
        P("expert", "dp", None),
    )
    return jax.shard_map(
        body,
        mesh=mesh,
        in_specs=placed,
        out_specs=(P(("groups", "expert"), "dp", None), P(("groups", "expert", "dp"), None)),
        check_vma=False,
    )
```

```python
import functools

import jax
import jax.numpy as jnp
from jax import lax
from jax.experimental import pallas as pl
from jax.experimental.pallas import tpu as pltpu
import numpy as np
from jax.sharding import PartitionSpec as P

MOST = 18
SUPER = 8
TILES = 9
GROUP = ("expert", "dp")
f32, bf16, i32 = jnp.float32, jnp.bfloat16, jnp.int32


SMEM = pl.BlockSpec(memory_space=pltpu.SMEM)
VMEM = pl.BlockSpec(memory_space=pltpu.VMEM)
ANYWHERE = pl.BlockSpec(memory_space=pl.ANY)


def dot(a, b, dims=((1,), (0,))):
    return lax.dot_general(a, b, (dims, ((), ())), preferred_element_type=f32)


def iota(shape, dim):
    return lax.broadcasted_iota(i32, shape, dim)


def params(megabytes):
    return pltpu.CompilerParams(vmem_limit_bytes=megabytes * 2**20)


def cost(flops, nbytes):
    return pl.CostEstimate(flops=int(flops), bytes_accessed=int(nbytes), transcendentals=0)


def token_slots(routes_t, experts):
    top_k, tok = routes_t.shape
    numbers = iota((experts, tok), 0)
    named = jnp.zeros((experts, tok), f32)
    for k in range(top_k):
        named += jnp.where(routes_t[k : k + 1, :] == numbers, 1.0, 0.0)
    before = jnp.where(iota((tok, tok), 0) < iota((tok, tok), 1), 1.0, 0.0)
    return named, dot(named.astype(bf16), before.astype(bf16))


def pack_kernel(n_dp, half, routes_t, routes_flat, weights_flat, hidden, early, out, copies, target):
    del early
    ex = pl.program_id(0)
    experts = pl.num_programs(0) * 2 * half // MOST
    n_routes = routes_flat.shape[1]
    top_k, tok = routes_t.shape
    part = hidden.shape[1] // n_dp
    copies[...] = jnp.broadcast_to(routes_t[...][None], copies.shape)

    @pl.when(ex == 0)
    def _():
        _, slots = token_slots(routes_t[...], experts)
        shape = (tok, n_routes)
        spread = jnp.where(iota(shape, 1) // top_k == iota(shape, 0), 1.0, 0.0)
        slots = dot(slots.astype(bf16), spread.astype(bf16))
        numbers = iota((experts, n_routes), 0)
        rows = slots + (numbers * MOST).astype(f32)
        rows = jnp.where(routes_flat[...] == numbers, rows, 0.0)
        target[...] = jnp.sum(rows, axis=0, keepdims=True).astype(i32)

    weights = weights_flat[...].astype(f32)
    for side in range(2):
        first = ex * 2 * half + side * half
        chosen = target[...] - first == iota((half, n_routes), 0)
        chosen = jnp.where(chosen, weights, 0.0).astype(bf16)
        rows = dot(chosen, hidden[...]).astype(bf16)
        for d in range(n_dp):
            out[d, :, side * part : (side + 1) * part] = rows[:, d * part : (d + 1) * part]


def pack(routes_t, routes_flat, weights_flat, hidden, early, n_expert, n_dp, half):
    n_routes, units = hidden.shape
    part = units // n_dp
    whole = lambda shape: pl.BlockSpec(shape, lambda i: (0,) * len(shape))
    return pl.pallas_call(
        functools.partial(pack_kernel, n_dp, half),
        grid=(n_expert,),
        in_specs=[
            whole(routes_t.shape),
            whole(routes_flat.shape),
            whole(weights_flat.shape),
            whole(hidden.shape),
            pl.BlockSpec(memory_space=pl.ANY),
        ],
        out_specs=[
            pl.BlockSpec((n_dp, half, 2 * part), lambda i: (i, 0, 0)),
            pl.BlockSpec((n_dp,) + routes_t.shape, lambda i: (i, 0, 0)),
        ],
        out_shape=[
            jax.ShapeDtypeStruct((n_expert * n_dp, half, 2 * part), bf16),
            jax.ShapeDtypeStruct((n_expert * n_dp,) + routes_t.shape, i32),
        ],
        scratch_shapes=[pltpu.VMEM((1, n_routes), i32)],
        compiler_params=params(16),
        cost_estimate=cost(4 * n_expert * half * n_routes * units, 6 * n_routes * units),
    )(routes_t, routes_flat, weights_flat, hidden, early)


def after_kernel(*refs):
    pass


def after(array, *events):
    anywhere = pl.BlockSpec(memory_space=pl.ANY)
    return pl.pallas_call(
        after_kernel,
        in_specs=[anywhere] * (1 + len(events)),
        out_specs=anywhere,
        out_shape=jax.ShapeDtypeStruct(array.shape, array.dtype),
        input_output_aliases={0: 0},
    )(array, *events)


def tile_rows(i, rows):
    first = min(16 * i // MOST, SUPER - 2)
    place = 16 * i + iota((rows, 1), 0) % 16
    second = place >= MOST * (first + 1)
    slot = place - MOST * first - jnp.where(second, MOST, 0)
    return first, second, slot


def block_at(place, order, index):
    return place[0] ^ order[index] if order else pl.program_id(0) * SUPER + index


def gather_rows(order, place, routes_t, grads, out, start=0):
    tok = routes_t.shape[2]
    ex_local, _, width = out.shape
    rows = 16 * ex_local
    slots = []
    for b in range(SUPER):
        mine = routes_t[block_at(place, order, b)] - place[1]
        named, before = token_slots(mine, ex_local)
        slots.append(jnp.where(named > 0, before, -1.0))
    shape = (rows, ex_local)
    spread = jnp.where(iota(shape, 0) // 16 == iota(shape, 1), 1.0, 0.0).astype(bf16)
    step = min(512, width)
    for i in range(TILES):
        first, second, slot = tile_rows(i, rows)
        pair = jnp.concatenate([slots[first], slots[first + 1]], axis=1)
        pair = dot(spread, pair.astype(bf16))
        slot = slot.astype(f32)
        wanted = jnp.where(
            iota((rows, 2 * tok), 1) < tok,
            jnp.where(second, -5.0, slot),
            jnp.where(second, slot, -5.0),
        )
        chosen = jnp.where(pair == wanted, 1.0, 0.0).astype(bf16)
        near, far = grads(first), grads(first + 1)
        tile = start + 16 * i
        for c in range(0, width, step):
            here = slice(c, c + step)
            both = jnp.concatenate([near[:, here], far[:, here]], axis=0)
            found = dot(chosen, both).astype(bf16).reshape(ex_local, 16, step)
            out[:, tile : tile + 16, here] = found


def gather_kernel(place, routes_t, *refs):
    gather_rows(None, place, routes_t, lambda b: refs[b], refs[SUPER])


def gather(place, routes_t, grads, ex_local):
    blocks, top_k, tok = routes_t.shape
    width = grads.shape[1]
    tall = SUPER * MOST
    picked = lambda j: pl.BlockSpec((tok, width), lambda s: (SUPER * s + j, 0))
    return pl.pallas_call(
        gather_kernel,
        grid=(blocks // SUPER,),
        in_specs=[SMEM, pl.BlockSpec(routes_t.shape, lambda s: (0, 0, 0))]
        + [picked(j) for j in range(SUPER)],
        out_specs=pl.BlockSpec((ex_local, tall, width), lambda s: (0, s, 0)),
        out_shape=jax.ShapeDtypeStruct((ex_local, blocks * MOST, width), bf16),
        compiler_params=params(48),
    )(place, routes_t, *([grads] * SUPER))


def fetch(sources, held, sems):
    copies = [[] for _ in range(held.shape[0])]
    rows = held.shape[1]
    for n, source in enumerate(sources):
        i = next(i for i, parts in enumerate(copies) if sum(p for p, _ in parts) < rows)
        filled = sum(size for size, _ in copies[i])
        size = source.shape[0]
        target = held.at[i, pl.ds(filled, size)]
        copy = pltpu.make_async_copy(source, target, sems.at[n])
        copies[i].append((size, copy))
        copy.start()
    waited = set()

    def block(i):
        if i not in waited:
            for _, copy in copies[i]:
                copy.wait()
            waited.add(i)
        return held.at[i]

    return block


def arrange_kernel(orders, ex_local, place, received, out):
    _, half, double = received.shape
    part = double // 2
    paired = ex_local % 2 == 0
    some = ex_local // 2 if paired else ex_local
    rows = 16 * some
    expert = iota((rows, 1), 0) // 16
    for i in range(TILES):
        first, second, slot = tile_rows(i, rows)
        block = jnp.where(second, half, 0)
        chosen = []
        for side in range(1 if paired else 2):
            spot = expert * MOST + slot - side * half
            column = jnp.where((spot >= 0) & (spot < half), block + spot, -1)
            hit = iota((rows, 2 * half), 1) == column
            chosen.append(jnp.where(hit, 1.0, 0.0).astype(bf16))
        for piece, order in enumerate(orders):
            pair = [received[block_at(place, order, first + b)] for b in range(2)]
            pair = jnp.concatenate(pair, axis=0)
            results = [dot(c, pair) for c in chosen]
            if paired:
                sides = [results[0][:, :part], results[0][:, part:]]
            else:
                sides = [results[0][:, :part] + results[1][:, part:]]
            tile = piece * SUPER * MOST + 16 * i
            for s, found in enumerate(sides):
                here = slice(s * some, (s + 1) * some)
                out[here, tile : tile + 16, :] = found.astype(bf16).reshape(some, 16, part)


def arrange(place, orders, received, ex_local):
    blocks, half, double = received.shape
    part = double // 2
    shape = (ex_local, blocks * MOST, part)
    kernel = functools.partial(arrange_kernel, orders, ex_local)
    if orders[0]:
        return pl.pallas_call(
            kernel,
            in_specs=[SMEM, VMEM],
            out_specs=VMEM,
            out_shape=jax.ShapeDtypeStruct(shape, bf16),
            compiler_params=params(24),
            cost_estimate=cost(4 * ex_local * blocks * MOST * half * double, 2**22),
        )(place, received)
    return pl.pallas_call(
        kernel,
        grid=(blocks // SUPER,),
        in_specs=[SMEM, pl.BlockSpec(received.shape, lambda s: (0, 0, 0))],
        out_specs=pl.BlockSpec((ex_local, SUPER * MOST, part), lambda s: (0, s, 0)),
        out_shape=jax.ShapeDtypeStruct(shape, bf16),
        compiler_params=params(32),
    )(place, received)


def back_rows(place, expert, hidden, grads, weights, sums):
    found = dot(grads, weights, ((1,), (1,)))
    total = jnp.sum(hidden.astype(f32) * found, axis=1, keepdims=True)
    sums[...] += jnp.where(iota(sums.shape, 1) == place[1] + expert, total, 0.0)


def back_kernel(place, hidden, grads, weights, out, sums):
    expert = pl.program_id(1)

    @pl.when(expert == 0)
    def _():
        sums[...] = jnp.zeros_like(sums)

    back_rows(place, expert, hidden[0], grads[0], weights[0], sums)

    @pl.when(expert == pl.num_programs(1) - 1)
    def _():
        for b in range(SUPER):
            out[b] = sums[b * MOST : (b + 1) * MOST, :]


def back(place, hidden, grads, weights):
    ex_local, rows, width = grads.shape
    part = weights.shape[1]
    tall = SUPER * MOST
    return pl.pallas_call(
        back_kernel,
        grid=(rows // tall, ex_local),
        in_specs=[
            SMEM,
            pl.BlockSpec((1, tall, part), lambda s, e: (e, s, 0)),
            pl.BlockSpec((1, tall, width), lambda s, e: (e, s, 0)),
            pl.BlockSpec((1, part, width), lambda s, e: (e, 0, 0)),
        ],
        out_specs=pl.BlockSpec((SUPER, MOST, 128), lambda s, e: (s, 0, 0)),
        out_shape=jax.ShapeDtypeStruct((rows // MOST, MOST, 128), f32),
        scratch_shapes=[pltpu.VMEM((tall, 128), f32)],
        compiler_params=params(32),
    )(place, hidden, grads, weights)


def early_kernel(order, place, routes_t, weights, *refs):
    blocks, (out, kept_rows, held, rows, sems) = refs[:SUPER], refs[SUPER:]
    step = pl.program_id(0)

    @pl.when(step == 0)
    def _():
        gather_rows(order, place, routes_t, fetch(blocks, held, sems), rows)

    for j in range(GROUPED):
        mine = rows[step * GROUPED + j]
        kept_rows[j] = mine
        out[j] = dot(mine, weights[j], ((1,), (1,)))


def early_products(place, order, routes_t, weights, blocks):
    ex_local, part, width = weights.shape
    tok = blocks[0].shape[0]
    tall = SUPER * MOST
    grouped = lambda rows, columns: pl.BlockSpec((GROUPED, rows, columns), lambda e: (e, 0, 0))
    return pl.pallas_call(
        functools.partial(early_kernel, order),
        grid=(ex_local // GROUPED,),
        in_specs=[SMEM, VMEM, grouped(part, width)] + [ANYWHERE] * SUPER,
        out_specs=[grouped(tall, part), grouped(tall, width)],
        out_shape=[
            jax.ShapeDtypeStruct((ex_local, tall, part), f32),
            jax.ShapeDtypeStruct((ex_local, tall, width), bf16),
        ],
        scratch_shapes=[
            pltpu.VMEM((SUPER, tok, width), bf16),
            pltpu.VMEM((ex_local, tall, width), bf16),
            pltpu.SemaphoreType.DMA((SUPER,)),
        ],
        compiler_params=params(40),
        cost_estimate=cost(
            2 * ex_local * tall * width * (part + 2 * tok), 2 * ex_local * part * width
        ),
    )(place, routes_t, weights, *blocks)


GROUPED = 4


def gradients_kernel(orders, place, routes_t, weights, hidden, backs, early, *refs):
    count = len(refs) - 6
    blocks, (out, summed, sums, held, rows, sems) = refs[:count], refs[count:]
    step = pl.program_id(0)
    tall = SUPER * MOST
    width = out.shape[2]
    columns = min(512, width)

    @pl.when(step == 0)
    def _():
        sums[...] = jnp.zeros_like(sums)
        gather_rows(orders[1], place, routes_t, fetch(blocks, held, sems), rows)

    lane = iota((tall, 128), 1) - place[1]
    for j in range(GROUPED):
        expert = step * GROUPED + j
        found = hidden[j, :tall, :].astype(f32) * backs[j]
        total = jnp.sum(found, axis=1, keepdims=True)
        sums[:tall, :] += jnp.where(lane == expert, total, 0.0)
        late = hidden[j, tall:, :]
        found = jnp.zeros((tall, 128), f32)
        for c in range(0, width, columns):
            here = slice(c, c + columns)
            mine = rows[expert, :, here]
            both = jnp.concatenate([early[j, :, here], mine], axis=0)
            product = dot(hidden[j], both, ((0,), (0,)))
            out[j, :, here] = product.astype(bf16)
            part = dot(late, weights[j, :, here]) * mine.astype(f32)
            for piece in range(0, columns, 128):
                found += part[:, piece : piece + 128]
        total = jnp.sum(found, axis=1, keepdims=True)
        sums[tall:, :] += jnp.where(lane == expert, total, 0.0)

    @pl.when(step == pl.num_programs(0) - 1)
    def _():
        for i, order in enumerate(orders):
            for b in range(SUPER):
                start = (i * SUPER + b) * MOST
                summed[block_at(place, order, b)] = sums[start : start + MOST, :]


def gradients(place, orders, routes_t, weights, hidden, backs, early, blocks):
    ex_local, part, width = weights.shape
    rows = hidden.shape[1]
    tok = blocks[0].shape[0]
    tall = SUPER * MOST
    count = 2 * SUPER
    sources = len(blocks)
    grouped = lambda rows, columns: pl.BlockSpec((GROUPED, rows, columns), lambda e: (e, 0, 0))
    return pl.pallas_call(
        functools.partial(gradients_kernel, orders),
        grid=(ex_local // GROUPED,),
        in_specs=[
            SMEM,
            VMEM,
            grouped(part, width),
            grouped(rows, part),
            grouped(tall, part),
            grouped(tall, width),
        ]
        + [ANYWHERE] * sources,
        out_specs=[
            grouped(part, width),
            pl.BlockSpec((count, MOST, 128), lambda e: (0, 0, 0)),
        ],
        out_shape=[
            jax.ShapeDtypeStruct((ex_local, part, width), bf16),
            jax.ShapeDtypeStruct((count, MOST, 128), f32),
        ],
        scratch_shapes=[
            pltpu.VMEM((rows, 128), f32),
            pltpu.VMEM((SUPER, tok, width), bf16),
            pltpu.VMEM((ex_local, tall, width), bf16),
            pltpu.SemaphoreType.DMA((sources,)),
        ],
        compiler_params=params(56),
        cost_estimate=cost(
            2 * ex_local * rows * width * (2 * part + 2 * tok), 4 * ex_local * part * width
        ),
    )(place, routes_t, weights, hidden, backs, early, *blocks)


def outer_kernel(hidden, grads, out, total):
    chunk = pl.program_id(1)

    @pl.when(chunk == 0)
    def _():
        total[...] = jnp.zeros_like(total)

    total[...] += dot(hidden[0], grads[0], ((0,), (0,)))

    @pl.when(chunk == pl.num_programs(1) - 1)
    def _():
        out[0] = total[...].astype(bf16)


def outer(hidden, grads):
    ex_local, rows, part = hidden.shape
    width = grads.shape[2]
    tall = SUPER * MOST
    return pl.pallas_call(
        outer_kernel,
        grid=(ex_local, rows // tall),
        in_specs=[
            pl.BlockSpec((1, tall, part), lambda e, c: (e, c, 0)),
            pl.BlockSpec((1, tall, width), lambda e, c: (e, c, 0)),
        ],
        out_specs=pl.BlockSpec((1, part, width), lambda e, c: (e, 0, 0)),
        out_shape=jax.ShapeDtypeStruct((ex_local, part, width), bf16),
        scratch_shapes=[pltpu.VMEM((part, width), f32)],
        compiler_params=params(32),
    )(hidden, grads)


def finish_kernel(experts, routes_t, weights_t, returned, out):
    top_k, tok = routes_t.shape
    total = jnp.sum(returned[...], axis=0)
    total = jnp.concatenate([total, jnp.zeros((128 - MOST, 128), f32)], axis=0)
    total = total.T[:experts]
    _, slots = token_slots(routes_t[...], experts)
    slots = slots.astype(i32)
    found = jnp.zeros((experts, tok), f32)
    for m in range(MOST):
        found = jnp.where(slots == m, total[:, m : m + 1], found)
    numbers = iota((experts, tok), 0)
    for k in range(top_k):
        mine = jnp.where(routes_t[k : k + 1, :] == numbers, found, 0.0)
        mine = jnp.sum(mine, axis=0, keepdims=True)
        out[k : k + 1, :] = mine / weights_t[k : k + 1, :].astype(f32)


def finish(routes_t, weights_t, returned, experts):
    return pl.pallas_call(
        functools.partial(finish_kernel, experts),
        out_shape=jax.ShapeDtypeStruct(routes_t.shape, f32),
        compiler_params=params(24),
        cost_estimate=cost(10000, 100000),
    )(routes_t, weights_t, returned)


def hop(block, axis, flip):
    size = lax.axis_size(axis)
    return lax.ppermute(block, axis, [(i, i ^ flip) for i in range(size)])


def body(routes, combine, hidden, d_out, w_down):
    n_expert = lax.axis_size("expert")
    n_dp = lax.axis_size("dp")
    ex_local = w_down.shape[0]
    experts = n_expert * ex_local
    tok, top_k = routes.shape
    half = ex_local * MOST // 2
    routes_t, weights_t = routes.T, combine.T
    n_routes = tok * top_k
    me, mine = lax.axis_index("expert") * n_dp + lax.axis_index("dp"), lax.axis_index("expert")
    place = jnp.stack([me, mine * ex_local]).astype(i32)
    small = (n_expert, n_dp) == (4, 4)
    trade = lambda x: lax.all_to_all(x, GROUP, split_axis=0, concat_axis=0, tiled=True)
    if small:
        near = hop(d_out, "expert", 1)
        side = hop(d_out, "dp", 2)
        far = hop(d_out, "expert", 2)
        twin = hop(d_out, "dp", 1)
    else:
        twin = d_out
    sent, copies = pack(
        routes_t,
        routes.reshape(1, n_routes),
        combine.reshape(1, n_routes),
        hidden.reshape(n_routes, hidden.shape[2]),
        twin,
        n_expert,
        n_dp,
        half,
    )
    all_routes = trade(copies)
    if small:
        near_twin, side_twin, far_twin = [hop(x, "dp", 1) for x in (near, side, far)]
        early = [(0, d_out), (4, near), (2, side), (8, far)]
        early += [(1, twin), (5, near_twin), (3, side_twin), (9, far_twin)]
        near_side = hop(near, "dp", 2)
        far_side = hop(far, "dp", 2)
        both = hop(far, "expert", 1)
        received = trade(after(sent, near, side, far))
        orders = [[n for n, _ in early], [6, 10, 12, 14, 7, 11, 13, 15]]
        early = [x for _, x in early]
        backs, rows = early_products(place, orders[0], all_routes, w_down, early)
        both, far_side = after(both, backs), after(far_side, backs)
        middle = tok // 2
        upper = hop(both[:middle], "dp", 2)
        lower = hop(far_side[middle:], "expert", 1)
        arranged = arrange(place, orders, received, ex_local)
        late = [near_side, far_side, both, after(upper, arranged), lower]
        late += [hop(x, "dp", 1) for x in late]
        d_w_down, sums = gradients(
            place, orders, all_routes, w_down, arranged, backs, rows, late
        )
    else:
        received = trade(sent)
        grads = lax.all_gather(d_out, GROUP, axis=0, tiled=True)
        grads = gather(place, all_routes, grads, ex_local)
        arranged = arrange(place, [None], received, ex_local)
        sums = back(place, arranged, grads, w_down)
        d_w_down = outer(arranged, grads)
    d_combine = finish(routes_t, weights_t, trade(sums), experts)
    return d_w_down, d_combine.T


def solution(mesh):
    placed = (
        P(("groups", "expert", "dp"), None),
        P(("groups", "expert", "dp"), None),
        P(("groups", "expert", "dp"), None, None),
        P(("groups", "expert", "dp"), None),
        P("expert", "dp", None),
    )
    return jax.shard_map(
        body,
        mesh=mesh,
        in_specs=placed,
        out_specs=(P(("groups", "expert"), "dp", None), P(("groups", "expert", "dp"), None)),
        check_vma=False,
    )
```

```python
import functools

import jax
import jax.numpy as jnp
from jax import lax
from jax.experimental import pallas as pl
from jax.experimental.pallas import tpu as pltpu
import numpy as np
from jax.sharding import PartitionSpec as P

MOST = 18
SUPER = 8
TILES = 9
GROUP = ("expert", "dp")
f32, bf16, i32 = jnp.float32, jnp.bfloat16, jnp.int32


SMEM = pl.BlockSpec(memory_space=pltpu.SMEM)
VMEM = pl.BlockSpec(memory_space=pltpu.VMEM)
ANYWHERE = pl.BlockSpec(memory_space=pl.ANY)


def dot(a, b, dims=((1,), (0,))):
    return lax.dot_general(a, b, (dims, ((), ())), preferred_element_type=f32)


def iota(shape, dim):
    return lax.broadcasted_iota(i32, shape, dim)


def params(megabytes):
    return pltpu.CompilerParams(vmem_limit_bytes=megabytes * 2**20)


def cost(flops, nbytes):
    return pl.CostEstimate(flops=int(flops), bytes_accessed=int(nbytes), transcendentals=0)


def token_slots(routes_t, experts):
    top_k, tok = routes_t.shape
    numbers = iota((experts, tok), 0)
    named = jnp.zeros((experts, tok), f32)
    for k in range(top_k):
        named += jnp.where(routes_t[k : k + 1, :] == numbers, 1.0, 0.0)
    before = jnp.where(iota((tok, tok), 0) < iota((tok, tok), 1), 1.0, 0.0)
    return named, dot(named.astype(bf16), before.astype(bf16))


def pack_kernel(n_dp, half, routes_t, routes_flat, weights_flat, hidden, early, out, copies, target):
    del early
    ex = pl.program_id(0)
    experts = pl.num_programs(0) * 2 * half // MOST
    n_routes = routes_flat.shape[1]
    top_k, tok = routes_t.shape
    part = hidden.shape[1] // n_dp
    copies[...] = jnp.broadcast_to(routes_t[...][None], copies.shape)

    @pl.when(ex == 0)
    def _():
        _, slots = token_slots(routes_t[...], experts)
        shape = (tok, n_routes)
        spread = jnp.where(iota(shape, 1) // top_k == iota(shape, 0), 1.0, 0.0)
        slots = dot(slots.astype(bf16), spread.astype(bf16))
        numbers = iota((experts, n_routes), 0)
        rows = slots + (numbers * MOST).astype(f32)
        rows = jnp.where(routes_flat[...] == numbers, rows, 0.0)
        target[...] = jnp.sum(rows, axis=0, keepdims=True).astype(i32)

    weights = weights_flat[...].astype(f32)
    for side in range(2):
        first = ex * 2 * half + side * half
        chosen = target[...] - first == iota((half, n_routes), 0)
        chosen = jnp.where(chosen, weights, 0.0).astype(bf16)
        rows = dot(chosen, hidden[...]).astype(bf16)
        for d in range(n_dp):
            out[d, :, side * part : (side + 1) * part] = rows[:, d * part : (d + 1) * part]


def pack(routes_t, routes_flat, weights_flat, hidden, early, n_expert, n_dp, half):
    n_routes, units = hidden.shape
    part = units // n_dp
    whole = lambda shape: pl.BlockSpec(shape, lambda i: (0,) * len(shape))
    return pl.pallas_call(
        functools.partial(pack_kernel, n_dp, half),
        grid=(n_expert,),
        in_specs=[
            whole(routes_t.shape),
            whole(routes_flat.shape),
            whole(weights_flat.shape),
            whole(hidden.shape),
            pl.BlockSpec(memory_space=pl.ANY),
        ],
        out_specs=[
            pl.BlockSpec((n_dp, half, 2 * part), lambda i: (i, 0, 0)),
            pl.BlockSpec((n_dp,) + routes_t.shape, lambda i: (i, 0, 0)),
        ],
        out_shape=[
            jax.ShapeDtypeStruct((n_expert * n_dp, half, 2 * part), bf16),
            jax.ShapeDtypeStruct((n_expert * n_dp,) + routes_t.shape, i32),
        ],
        scratch_shapes=[pltpu.VMEM((1, n_routes), i32)],
        compiler_params=params(16),
        cost_estimate=cost(4 * n_expert * half * n_routes * units, 6 * n_routes * units),
    )(routes_t, routes_flat, weights_flat, hidden, early)


def after_kernel(*refs):
    pass


def after(array, *events):
    anywhere = pl.BlockSpec(memory_space=pl.ANY)
    return pl.pallas_call(
        after_kernel,
        in_specs=[anywhere] * (1 + len(events)),
        out_specs=anywhere,
        out_shape=jax.ShapeDtypeStruct(array.shape, array.dtype),
        input_output_aliases={0: 0},
    )(array, *events)


def tile_rows(i, rows):
    first = min(16 * i // MOST, SUPER - 2)
    place = 16 * i + iota((rows, 1), 0) % 16
    second = place >= MOST * (first + 1)
    slot = place - MOST * first - jnp.where(second, MOST, 0)
    return first, second, slot


def block_at(place, order, index):
    return place[0] ^ order[index] if order else pl.program_id(0) * SUPER + index


def gather_rows(order, place, routes_t, grads, out, start=0):
    tok = routes_t.shape[2]
    ex_local, _, width = out.shape
    rows = 16 * ex_local
    slots = []
    for b in range(SUPER):
        mine = routes_t[block_at(place, order, b)] - place[1]
        named, before = token_slots(mine, ex_local)
        slots.append(jnp.where(named > 0, before, -1.0))
    shape = (rows, ex_local)
    spread = jnp.where(iota(shape, 0) // 16 == iota(shape, 1), 1.0, 0.0).astype(bf16)
    step = min(512, width)
    for i in range(TILES):
        first, second, slot = tile_rows(i, rows)
        pair = jnp.concatenate([slots[first], slots[first + 1]], axis=1)
        pair = dot(spread, pair.astype(bf16))
        slot = slot.astype(f32)
        wanted = jnp.where(
            iota((rows, 2 * tok), 1) < tok,
            jnp.where(second, -5.0, slot),
            jnp.where(second, slot, -5.0),
        )
        chosen = jnp.where(pair == wanted, 1.0, 0.0).astype(bf16)
        near, far = grads(first), grads(first + 1)
        tile = start + 16 * i
        for c in range(0, width, step):
            here = slice(c, c + step)
            both = jnp.concatenate([near[:, here], far[:, here]], axis=0)
            found = dot(chosen, both).astype(bf16).reshape(ex_local, 16, step)
            out[:, tile : tile + 16, here] = found


def gather_kernel(place, routes_t, *refs):
    gather_rows(None, place, routes_t, lambda b: refs[b], refs[SUPER])


def gather(place, routes_t, grads, ex_local):
    blocks, top_k, tok = routes_t.shape
    width = grads.shape[1]
    tall = SUPER * MOST
    picked = lambda j: pl.BlockSpec((tok, width), lambda s: (SUPER * s + j, 0))
    return pl.pallas_call(
        gather_kernel,
        grid=(blocks // SUPER,),
        in_specs=[SMEM, pl.BlockSpec(routes_t.shape, lambda s: (0, 0, 0))]
        + [picked(j) for j in range(SUPER)],
        out_specs=pl.BlockSpec((ex_local, tall, width), lambda s: (0, s, 0)),
        out_shape=jax.ShapeDtypeStruct((ex_local, blocks * MOST, width), bf16),
        compiler_params=params(48),
    )(place, routes_t, *([grads] * SUPER))


def fetch(sources, held, sems):
    copies = [[] for _ in range(held.shape[0])]
    rows = held.shape[1]
    for n, source in enumerate(sources):
        i = next(i for i, parts in enumerate(copies) if sum(p for p, _ in parts) < rows)
        filled = sum(size for size, _ in copies[i])
        size = source.shape[0]
        target = held.at[i, pl.ds(filled, size)]
        copy = pltpu.make_async_copy(source, target, sems.at[n])
        copies[i].append((size, copy))
        copy.start()
    waited = set()

    def block(i):
        if i not in waited:
            for _, copy in copies[i]:
                copy.wait()
            waited.add(i)
        return held.at[i]

    return block


def arrange_kernel(orders, ex_local, place, received, out):
    _, half, double = received.shape
    part = double // 2
    paired = ex_local % 2 == 0
    some = ex_local // 2 if paired else ex_local
    rows = 16 * some
    expert = iota((rows, 1), 0) // 16
    for i in range(TILES):
        first, second, slot = tile_rows(i, rows)
        block = jnp.where(second, half, 0)
        chosen = []
        for side in range(1 if paired else 2):
            spot = expert * MOST + slot - side * half
            column = jnp.where((spot >= 0) & (spot < half), block + spot, -1)
            hit = iota((rows, 2 * half), 1) == column
            chosen.append(jnp.where(hit, 1.0, 0.0).astype(bf16))
        for piece, order in enumerate(orders):
            pair = [received[block_at(place, order, first + b)] for b in range(2)]
            pair = jnp.concatenate(pair, axis=0)
            results = [dot(c, pair) for c in chosen]
            if paired:
                sides = [results[0][:, :part], results[0][:, part:]]
            else:
                sides = [results[0][:, :part] + results[1][:, part:]]
            tile = piece * SUPER * MOST + 16 * i
            for s, found in enumerate(sides):
                here = slice(s * some, (s + 1) * some)
                out[here, tile : tile + 16, :] = found.astype(bf16).reshape(some, 16, part)


def arrange(place, orders, received, ex_local):
    blocks, half, double = received.shape
    part = double // 2
    shape = (ex_local, blocks * MOST, part)
    kernel = functools.partial(arrange_kernel, orders, ex_local)
    if orders[0]:
        return pl.pallas_call(
            kernel,
            in_specs=[SMEM, VMEM],
            out_specs=VMEM,
            out_shape=jax.ShapeDtypeStruct(shape, bf16),
            compiler_params=params(24),
            cost_estimate=cost(4 * ex_local * blocks * MOST * half * double, 2**22),
        )(place, received)
    return pl.pallas_call(
        kernel,
        grid=(blocks // SUPER,),
        in_specs=[SMEM, pl.BlockSpec(received.shape, lambda s: (0, 0, 0))],
        out_specs=pl.BlockSpec((ex_local, SUPER * MOST, part), lambda s: (0, s, 0)),
        out_shape=jax.ShapeDtypeStruct(shape, bf16),
        compiler_params=params(32),
    )(place, received)


def back_rows(place, expert, hidden, grads, weights, sums):
    found = dot(grads, weights, ((1,), (1,)))
    total = jnp.sum(hidden.astype(f32) * found, axis=1, keepdims=True)
    sums[...] += jnp.where(iota(sums.shape, 1) == place[1] + expert, total, 0.0)


def back_kernel(place, hidden, grads, weights, out, sums):
    expert = pl.program_id(1)

    @pl.when(expert == 0)
    def _():
        sums[...] = jnp.zeros_like(sums)

    back_rows(place, expert, hidden[0], grads[0], weights[0], sums)

    @pl.when(expert == pl.num_programs(1) - 1)
    def _():
        for b in range(SUPER):
            out[b] = sums[b * MOST : (b + 1) * MOST, :]


def back(place, hidden, grads, weights):
    ex_local, rows, width = grads.shape
    part = weights.shape[1]
    tall = SUPER * MOST
    return pl.pallas_call(
        back_kernel,
        grid=(rows // tall, ex_local),
        in_specs=[
            SMEM,
            pl.BlockSpec((1, tall, part), lambda s, e: (e, s, 0)),
            pl.BlockSpec((1, tall, width), lambda s, e: (e, s, 0)),
            pl.BlockSpec((1, part, width), lambda s, e: (e, 0, 0)),
        ],
        out_specs=pl.BlockSpec((SUPER, MOST, 128), lambda s, e: (s, 0, 0)),
        out_shape=jax.ShapeDtypeStruct((rows // MOST, MOST, 128), f32),
        scratch_shapes=[pltpu.VMEM((tall, 128), f32)],
        compiler_params=params(32),
    )(place, hidden, grads, weights)


def early_kernel(order, place, routes_t, weights, *refs):
    blocks, (out, kept_rows, held, rows, sems) = refs[:SUPER], refs[SUPER:]
    step = pl.program_id(0)

    @pl.when(step == 0)
    def _():
        gather_rows(order, place, routes_t, fetch(blocks, held, sems), rows)

    for j in range(GROUPED):
        mine = rows[step * GROUPED + j]
        kept_rows[j] = mine
        out[j] = dot(mine, weights[j], ((1,), (1,)))


def early_products(place, order, routes_t, weights, blocks):
    ex_local, part, width = weights.shape
    tok = blocks[0].shape[0]
    tall = SUPER * MOST
    grouped = lambda rows, columns: pl.BlockSpec((GROUPED, rows, columns), lambda e: (e, 0, 0))
    return pl.pallas_call(
        functools.partial(early_kernel, order),
        grid=(ex_local // GROUPED,),
        in_specs=[SMEM, VMEM, grouped(part, width)] + [ANYWHERE] * SUPER,
        out_specs=[grouped(tall, part), grouped(tall, width)],
        out_shape=[
            jax.ShapeDtypeStruct((ex_local, tall, part), f32),
            jax.ShapeDtypeStruct((ex_local, tall, width), bf16),
        ],
        scratch_shapes=[
            pltpu.VMEM((SUPER, tok, width), bf16),
            pltpu.VMEM((ex_local, tall, width), bf16),
            pltpu.SemaphoreType.DMA((SUPER,)),
        ],
        compiler_params=params(40),
        cost_estimate=cost(
            2 * ex_local * tall * width * (part + 2 * tok), 2 * ex_local * part * width
        ),
    )(place, routes_t, weights, *blocks)


GROUPED = 4


def gradients_kernel(orders, place, routes_t, weights, hidden, backs, early, *refs):
    count = len(refs) - 6
    blocks, (out, summed, sums, held, rows, sems) = refs[:count], refs[count:]
    step = pl.program_id(0)
    tall = SUPER * MOST
    width = out.shape[2]
    columns = min(1024, width)

    @pl.when(step == 0)
    def _():
        sums[...] = jnp.zeros_like(sums)
        gather_rows(orders[1], place, routes_t, fetch(blocks, held, sems), rows)

    lane = iota((tall, 128), 1) - place[1]
    for j in range(GROUPED):
        expert = step * GROUPED + j
        found = hidden[j, :tall, :].astype(f32) * backs[j]
        total = jnp.sum(found, axis=1, keepdims=True)
        sums[:tall, :] += jnp.where(lane == expert, total, 0.0)
        late = hidden[j, tall:, :]
        found = jnp.zeros((tall, 128), f32)
        for c in range(0, width, columns):
            here = slice(c, c + columns)
            mine = rows[expert, :, here]
            both = jnp.concatenate([early[j, :, here], mine], axis=0)
            product = dot(hidden[j], both, ((0,), (0,)))
            out[j, :, here] = product.astype(bf16)
            part = dot(late, weights[j, :, here]) * mine.astype(f32)
            for piece in range(0, columns, 128):
                found += part[:, piece : piece + 128]
        total = jnp.sum(found, axis=1, keepdims=True)
        sums[tall:, :] += jnp.where(lane == expert, total, 0.0)

    @pl.when(step == pl.num_programs(0) - 1)
    def _():
        for i, order in enumerate(orders):
            for b in range(SUPER):
                start = (i * SUPER + b) * MOST
                summed[block_at(place, order, b)] = sums[start : start + MOST, :]


def gradients(place, orders, routes_t, weights, hidden, backs, early, blocks):
    ex_local, part, width = weights.shape
    rows = hidden.shape[1]
    tok = blocks[0].shape[0]
    tall = SUPER * MOST
    count = 2 * SUPER
    sources = len(blocks)
    grouped = lambda rows, columns: pl.BlockSpec((GROUPED, rows, columns), lambda e: (e, 0, 0))
    return pl.pallas_call(
        functools.partial(gradients_kernel, orders),
        grid=(ex_local // GROUPED,),
        in_specs=[
            SMEM,
            VMEM,
            grouped(part, width),
            grouped(rows, part),
            grouped(tall, part),
            grouped(tall, width),
        ]
        + [ANYWHERE] * sources,
        out_specs=[
            grouped(part, width),
            pl.BlockSpec((count, MOST, 128), lambda e: (0, 0, 0)),
        ],
        out_shape=[
            jax.ShapeDtypeStruct((ex_local, part, width), bf16),
            jax.ShapeDtypeStruct((count, MOST, 128), f32),
        ],
        scratch_shapes=[
            pltpu.VMEM((rows, 128), f32),
            pltpu.VMEM((SUPER, tok, width), bf16),
            pltpu.VMEM((ex_local, tall, width), bf16),
            pltpu.SemaphoreType.DMA((sources,)),
        ],
        compiler_params=params(56),
        cost_estimate=cost(
            2 * ex_local * rows * width * (2 * part + 2 * tok), 4 * ex_local * part * width
        ),
    )(place, routes_t, weights, hidden, backs, early, *blocks)


def outer_kernel(hidden, grads, out, total):
    chunk = pl.program_id(1)

    @pl.when(chunk == 0)
    def _():
        total[...] = jnp.zeros_like(total)

    total[...] += dot(hidden[0], grads[0], ((0,), (0,)))

    @pl.when(chunk == pl.num_programs(1) - 1)
    def _():
        out[0] = total[...].astype(bf16)


def outer(hidden, grads):
    ex_local, rows, part = hidden.shape
    width = grads.shape[2]
    tall = SUPER * MOST
    return pl.pallas_call(
        outer_kernel,
        grid=(ex_local, rows // tall),
        in_specs=[
            pl.BlockSpec((1, tall, part), lambda e, c: (e, c, 0)),
            pl.BlockSpec((1, tall, width), lambda e, c: (e, c, 0)),
        ],
        out_specs=pl.BlockSpec((1, part, width), lambda e, c: (e, 0, 0)),
        out_shape=jax.ShapeDtypeStruct((ex_local, part, width), bf16),
        scratch_shapes=[pltpu.VMEM((part, width), f32)],
        compiler_params=params(32),
    )(hidden, grads)


def finish_kernel(experts, routes_t, weights_t, returned, out):
    top_k, tok = routes_t.shape
    total = jnp.sum(returned[...], axis=0)
    total = jnp.concatenate([total, jnp.zeros((128 - MOST, 128), f32)], axis=0)
    total = total.T[:experts]
    _, slots = token_slots(routes_t[...], experts)
    slots = slots.astype(i32)
    found = jnp.zeros((experts, tok), f32)
    for m in range(MOST):
        found = jnp.where(slots == m, total[:, m : m + 1], found)
    numbers = iota((experts, tok), 0)
    for k in range(top_k):
        mine = jnp.where(routes_t[k : k + 1, :] == numbers, found, 0.0)
        mine = jnp.sum(mine, axis=0, keepdims=True)
        out[k : k + 1, :] = mine / weights_t[k : k + 1, :].astype(f32)


def finish(routes_t, weights_t, returned, experts):
    return pl.pallas_call(
        functools.partial(finish_kernel, experts),
        out_shape=jax.ShapeDtypeStruct(routes_t.shape, f32),
        compiler_params=params(24),
        cost_estimate=cost(10000, 100000),
    )(routes_t, weights_t, returned)


def hop(block, axis, flip):
    size = lax.axis_size(axis)
    return lax.ppermute(block, axis, [(i, i ^ flip) for i in range(size)])


def body(routes, combine, hidden, d_out, w_down):
    n_expert = lax.axis_size("expert")
    n_dp = lax.axis_size("dp")
    ex_local = w_down.shape[0]
    experts = n_expert * ex_local
    tok, top_k = routes.shape
    half = ex_local * MOST // 2
    routes_t, weights_t = routes.T, combine.T
    n_routes = tok * top_k
    me, mine = lax.axis_index("expert") * n_dp + lax.axis_index("dp"), lax.axis_index("expert")
    place = jnp.stack([me, mine * ex_local]).astype(i32)
    small = (n_expert, n_dp) == (4, 4)
    trade = lambda x: lax.all_to_all(x, GROUP, split_axis=0, concat_axis=0, tiled=True)
    if small:
        near = hop(d_out, "expert", 1)
        side = hop(d_out, "dp", 2)
        far = hop(d_out, "expert", 2)
        twin = hop(d_out, "dp", 1)
    else:
        twin = d_out
    sent, copies = pack(
        routes_t,
        routes.reshape(1, n_routes),
        combine.reshape(1, n_routes),
        hidden.reshape(n_routes, hidden.shape[2]),
        twin,
        n_expert,
        n_dp,
        half,
    )
    all_routes = trade(copies)
    if small:
        near_twin, side_twin, far_twin = [hop(x, "dp", 1) for x in (near, side, far)]
        early = [(0, d_out), (4, near), (2, side), (8, far)]
        early += [(1, twin), (5, near_twin), (3, side_twin), (9, far_twin)]
        near_side = hop(near, "dp", 2)
        far_side = hop(far, "dp", 2)
        both = hop(far, "expert", 1)
        received = trade(after(sent, near, side, far))
        orders = [[n for n, _ in early], [6, 10, 12, 14, 7, 11, 13, 15]]
        early = [x for _, x in early]
        backs, rows = early_products(place, orders[0], all_routes, w_down, early)
        both, far_side = after(both, backs), after(far_side, backs)
        middle = tok // 2
        upper = hop(both[:middle], "dp", 2)
        lower = hop(far_side[middle:], "expert", 1)
        arranged = arrange(place, orders, received, ex_local)
        late = [near_side, far_side, both, after(upper, arranged), lower]
        late += [hop(x, "dp", 1) for x in late]
        d_w_down, sums = gradients(
            place, orders, all_routes, w_down, arranged, backs, rows, late
        )
    else:
        received = trade(sent)
        grads = lax.all_gather(d_out, GROUP, axis=0, tiled=True)
        grads = gather(place, all_routes, grads, ex_local)
        arranged = arrange(place, [None], received, ex_local)
        sums = back(place, arranged, grads, w_down)
        d_w_down = outer(arranged, grads)
    d_combine = finish(routes_t, weights_t, trade(sums), experts)
    return d_w_down, d_combine.T


def solution(mesh):
    placed = (
        P(("groups", "expert", "dp"), None),
        P(("groups", "expert", "dp"), None),
        P(("groups", "expert", "dp"), None, None),
        P(("groups", "expert", "dp"), None),
        P("expert", "dp", None),
    )
    return jax.shard_map(
        body,
        mesh=mesh,
        in_specs=placed,
        out_specs=(P(("groups", "expert"), "dp", None), P(("groups", "expert", "dp"), None)),
        check_vma=False,
    )
```
